256 devices in a mesh: pool: 8 (over z), head: 32 (over y, x, core).
Axes of the slice: x: 4, y: 4, z: 8, core: 2. Of those that a mesh axis runs over, the one named last changes fastest.
Arguments:
- queries: bfloat16 [4096, 24576], P('pool', 'head'), may hold values from -8 to 8
- new_latent: bfloat16 [4096, 576], P('pool'), may hold values from -6 to 6
- latent_pool: bfloat16 [4096, 4608], P(('pool', 'head')), may hold values from -6 to 6
- w_ukv: bfloat16 [512, 32768], P(None, 'head'), may hold values from -0.25 to 0.25
- w_out: bfloat16 [16384, 7168], P('head'), may hold values from -0.375 to 0.375
- cached_len: int32 [8], replicated, may hold values from 1 to 2048, 5461 in all
- page_loc: int32 [8, 256], replicated, may hold values from 0 to 4095, as said below
Outputs:
- output: bfloat16 [4096, 7168], P('pool', 'head')
The draws below stay inside these ranges and needn't reach their ends.
Inputs may be any that keep to these rules, and one draw needn't show every extreme that they name: `page_loc`: page slot s of every request lies on a device whose head index is s mod 32 (the pool's pages are laid out device after device, 16 on each, devices in pool-major order); every device holds exactly 1 of the page slots of each request; no page is named twice.
All inputs are finite; a program needn't handle non-finite values.
Results may differ from the reference program's by a relative error of at most 0.02.
Values may be sent and summed in bfloat16 or wider, within the bound.
No kernel may reach another device: no remote copies, remote signals or barrier semaphores. Data moves between devices by JAX's collectives and lax.ppermute only.
A program may use at most 64 MiB of HBM per device.

```python
import math
from functools import partial
import jax
import jax.numpy as jnp
import numpy as np
from jax import lax

H = 128
NOPE = 128
ROPE = 64
VD = 128
KV = 512
D = 7168
NEW = 512
PAGE = 8
MAXP = 256
REQ = 8
TOKENS = 4096
HPD = 4
PREFIX = 2048
SLOTS = 8
CAP = 1
PAGES_DEV = 16
POOL_PAGES = 4096
N_POOL = 8
N_HEAD = 32


def draw_queries(key, part):
    key = jax.random.fold_in(key, 21)
    shape_full = (TOKENS, H, NOPE + ROPE)
    values = jax.random.truncated_normal(key, -6.0, 6.0, shape_full, jnp.float32)
    return values.reshape(TOKENS, H * (NOPE + ROPE)).astype(jnp.bfloat16)


def draw_latent_pool(key, part):
    key = jax.random.fold_in(key, 31)
    shape_full = (POOL_PAGES, PAGE, KV + ROPE)
    values = jax.random.truncated_normal(key, -6.0, 6.0, shape_full, jnp.float32)
    return values.reshape(POOL_PAGES, PAGE * (KV + ROPE)).astype(jnp.bfloat16)


def draw_page_loc(key, part):
    key = jax.random.fold_in(key, 41)
    key_order, key_shelf = jax.random.split(key)
    order_keys = jax.random.split(key_order, N_POOL * N_HEAD)
    orders = jax.vmap(partial(jax.random.permutation, x=SLOTS))(order_keys).reshape(N_POOL, N_HEAD, SLOTS)
    orders = jnp.transpose(orders, (0, 2, 1)).astype(jnp.int32)
    owners = orders // CAP
    within = orders % CAP
    shelf_keys = jax.random.split(key_shelf, N_POOL * N_HEAD)
    shelf = jax.vmap(partial(jax.random.permutation, x=PAGES_DEV))(shelf_keys).reshape(N_POOL, N_HEAD, PAGES_DEV).astype(jnp.int32)
    request_ids = jnp.arange(N_POOL, dtype=jnp.int32)[:, None, None]
    head_ids = jnp.arange(N_HEAD, dtype=jnp.int32)[None, None, :]
    local_pages = shelf[owners, head_ids, request_ids * CAP + within]
    global_ids = (owners * N_HEAD + head_ids) * PAGES_DEV + local_pages
    return global_ids.reshape(N_POOL, MAXP).astype(jnp.int32)


def shard_levels(own_key, dims, cuts, least, high):
    gain, own = 1.0, jax.random.fold_in(own_key, 6)
    for axis_at, shards_of in cuts:
        heights = jnp.exp(jax.random.uniform(jax.random.fold_in(own, axis_at), (shards_of,), jnp.float32, least / len(cuts), high / len(cuts)))
        gain = gain * jnp.repeat(heights, dims[axis_at] // shards_of).reshape([-1 if axis == axis_at else 1 for axis in range(len(dims))])
    return gain


def profile(count, total, reach, lean):
    weights = [(1 << 20) // math.isqrt(rank ** lean) + 1 for rank in range(2, count + 1)]
    surplus, holding = total - reach - (count - 1), [1] * (count - 1)
    while surplus > 0:
        movable = [i for i in range(count - 1) if holding[i] < reach]
        mass, remaining = sum([weights[i] for i in movable]), surplus
        for i in movable:
            more = min(reach - holding[i], max(1, remaining * weights[i] // mass), surplus)
            holding[i] = holding[i] + more
            surplus = surplus - more
    return np.array([reach] + holding)


def uneven_parts(own_key, amount, total, reach, lean):
    if amount == 2:
        one = jax.random.randint(own_key, (), max(1, total - reach), min(reach, total - 1) + 1)
        return jnp.stack([one, total - one])
    lengths = jnp.asarray(profile(amount, total, reach, lean), jnp.int32)
    twos = (amount - 1) // 2
    source_of, taker = lengths[1:1 + 2 * twos:2], lengths[2:2 + 2 * twos:2]
    margin = jnp.minimum(source_of - 1, reach - taker)
    shifted = jax.random.randint(jax.random.fold_in(own_key, 1), (twos,), 0, 1 << 20) % (margin + 1)
    lengths = lengths.at[1:1 + 2 * twos:2].set(source_of - shifted).at[2:2 + 2 * twos:2].set(taker + shifted)
    return lengths[jax.random.permutation(jax.random.fold_in(own_key, 2), amount)]


def gaussian(rng, extent, deviation, most, pieces=(), kind=jnp.bfloat16):
    array = deviation * jax.random.normal(rng, extent, jnp.float32)
    if pieces:
        array = array * shard_levels(rng, extent, pieces, -0.22, 0.18)
    return jnp.clip(array, -most, most).astype(kind)


def setup_inputs(seed: int = 0) -> dict:
    arg_keys = jax.random.split(jax.random.key(seed), 8)
    queries = draw_queries(jax.random.fold_in(arg_keys[7], 71), 0)
    new_latent = gaussian(arg_keys[1], (TOKENS, KV + ROPE), 1.0, 6.0, ((0, 8),))
    latent_pool = draw_latent_pool(jax.random.fold_in(arg_keys[7], 71), 0)
    w_ukv = gaussian(arg_keys[3], (KV, H * (NOPE + VD)), KV ** -0.5, 0.25, ((1, 32),))
    w_out = gaussian(arg_keys[4], (H * VD, D), (H * VD // 64) ** -0.5, 0.375, ((0, 32),))
    cached_len = uneven_parts(arg_keys[5], REQ, N_POOL * MAXP * PAGE // 3, MAXP * PAGE, 2).astype(jnp.int32)
    page_loc = draw_page_loc(jax.random.fold_in(arg_keys[7], 71), 0)
    return {"queries": queries, "new_latent": new_latent, "latent_pool": latent_pool, "w_ukv": w_ukv, "w_out": w_out, "cached_len": cached_len, "page_loc": page_loc}


def reference(queries, new_latent, latent_pool, w_ukv, w_out, cached_len, page_loc):
    latent_width = KV + ROPE
    page_rows = latent_pool.reshape(POOL_PAGES, PAGE, latent_width)
    score_scale = (NOPE + ROPE) ** -0.5
    key_count = PREFIX + NEW
    key_pos = jnp.arange(key_count, dtype=jnp.int32)[None, :]
    query_pos = jnp.arange(NEW, dtype=jnp.int32)[:, None]

    def one_request(request_args):
        page_table, length, query_rows, new_rows = request_args
        prefix = page_rows[page_table].reshape(PREFIX, latent_width)
        latent_all = jnp.concatenate([prefix, new_rows], 0)
        allowed = (key_pos < length) | ((key_pos >= PREFIX) & (key_pos - PREFIX <= query_pos))
        rope_keys = latent_all[:, KV:].astype(jnp.float32)
        query_heads = query_rows.reshape(NEW, H, NOPE + ROPE)

        def one_group(running, group):
            w_cols = lax.dynamic_slice_in_dim(w_ukv, group * HPD * (NOPE + VD), HPD * (NOPE + VD), 1)
            lifted = jnp.dot(latent_all[:, :KV], w_cols, preferred_element_type=jnp.float32)
            lifted = lifted.astype(jnp.bfloat16).reshape(key_count, HPD, NOPE + VD).astype(jnp.float32)
            group_query = lax.dynamic_slice_in_dim(query_heads, group * HPD, HPD, 1).astype(jnp.float32)
            scores = jnp.einsum('qhd,khd->hqk', group_query[..., :NOPE], lifted[..., :NOPE])
            scores = (scores + jnp.einsum('qhd,kd->hqk', group_query[..., NOPE:], rope_keys)) * score_scale
            scores = jnp.where(allowed[None], scores, -jnp.inf)
            row_max = jnp.max(scores, axis=2, keepdims=True)
            raised = jnp.exp(scores - row_max)
            weights = (raised / jnp.sum(raised, axis=2, keepdims=True)).astype(jnp.bfloat16)
            attended = jnp.einsum('hqk,khd->qhd', weights.astype(jnp.float32), lifted[..., NOPE:])
            attended = attended.astype(jnp.bfloat16).reshape(NEW, HPD * VD)
            w_rows = lax.dynamic_slice_in_dim(w_out, group * HPD * VD, HPD * VD, 0)
            partial_value = jnp.dot(attended, w_rows, preferred_element_type=jnp.float32)
            partial_value = lax.optimization_barrier(partial_value.astype(jnp.bfloat16)).astype(jnp.float32)
            return running + partial_value, None

        summed, unused = lax.scan(one_group, jnp.zeros((NEW, D), jnp.float32), jnp.arange(N_HEAD, dtype=jnp.int32))
        return summed.astype(jnp.bfloat16)

    result = lax.map(one_request, (page_loc, cached_len, queries.reshape(REQ, NEW, H * (NOPE + ROPE)), new_latent.reshape(REQ, NEW, latent_width)))
    return result.reshape(TOKENS, D)
```

```python
import functools

import jax
import jax.numpy as jnp
from jax import lax
from jax.experimental import pallas as pl
from jax.experimental.pallas import tpu as pltpu
from jax.sharding import PartitionSpec as P

NOPE = 128
ROPE = 64
VD = 128
KV = 512
NEW = 512
PAGE = 8
MAXP = 256
HPD = 4
REQ = 8
N_HEAD = 32
PAGES_DEV = 16
D = 7168
COLS = D // N_HEAD
WIDTH = KV + ROPE
PAY = KV + 128
HALF = NEW // 2
SIDE = 4
BLOCKED = -1e30
SCALE = (NOPE + ROPE) ** -0.5 * 1.4426950408889634
BF = jnp.bfloat16
F32 = jnp.float32
NT = (((1,), (1,)), ((), ()))
VMEM = pl.BlockSpec(memory_space=pltpu.VMEM)
SMEM = pl.BlockSpec(memory_space=pltpu.SMEM)


def head_index(y, x, c):
    return ((y % SIDE) * SIDE + x % SIDE) * 2 + c


def plane_perm(move):
    return [
        (head_index(y, x, c), head_index(*move(y, x, c)))
        for y in range(SIDE)
        for x in range(SIDE)
        for c in range(2)
    ]


SWAP = plane_perm(lambda y, x, c: (y, x, 1 - c))


def along_x(d):
    return plane_perm(lambda y, x, c: (y, x + d, c))


def along_y(d):
    return plane_perm(lambda y, x, c: (y + d, x, c))


def send(value, perm):
    return lax.ppermute(value, "head", perm)


def params(mib):
    return pltpu.CompilerParams(vmem_limit_bytes=mib << 20)


def cost(flops, nbytes, trans=0):
    return pl.CostEstimate(flops=flops, bytes_accessed=nbytes, transcendentals=trans)


def pages_kernel(place, lens, locs, pool_ref, out_ref, wide, rows):
    wide[...] = pool_ref[...].astype(F32)
    pool_id = place[0]
    head_id = place[1]
    lane = lax.broadcasted_iota(jnp.int32, (1, 128), 1)

    def one_request(r, carry):
        sel = jnp.int32(0)
        slot = jnp.int32(0)
        for i in range(MAXP // N_HEAD):
            loc = locs[r, head_id + i * N_HEAD]
            mine = lax.shift_right_logical(loc, 9) == pool_id
            sel = jnp.where(mine, loc & (PAGES_DEV - 1), sel)
            slot = jnp.where(mine, head_id + i * N_HEAD, slot)
        length = lens[r]
        for u in range(PAGE // 2):
            two = wide[pl.ds(sel, 1), 2 * WIDTH * u : 2 * WIDTH * (u + 1)]
            for odd in range(2):
                t = 2 * u + odd
                token = pltpu.roll(two, WIDTH, 1) if odd else two
                extra = jnp.where(slot * PAGE + t < length, 0.0, BLOCKED)
                tail = jnp.where(lane < ROPE, token[:, KV:PAY], jnp.where(lane == ROPE, extra, 0.0))
                rows[r, t : t + 1, :KV] = token[:, :KV]
                rows[r, t : t + 1, KV:] = tail
        return carry

    lax.fori_loop(0, REQ, one_request, 0)
    out_ref[...] = rows[...].astype(BF)


def own_pages(place, cached_len, page_loc, latent_pool):
    return pl.pallas_call(
        pages_kernel,
        out_shape=jax.ShapeDtypeStruct((REQ, PAGE, PAY), BF),
        in_specs=[SMEM, SMEM, SMEM, VMEM],
        out_specs=VMEM,
        scratch_shapes=[
            pltpu.VMEM((PAGES_DEV, PAGE * WIDTH), F32),
            pltpu.VMEM((REQ, PAGE, PAY), F32),
        ],
        compiler_params=params(8),
        cost_estimate=cost(0, 1 << 20),
        name="own_pages",
    )(place, cached_len, page_loc, latent_pool)


def new_kernel(q_ref, lat_ref, w_ref, q_out, kv_out, rope_out):
    lane = lax.broadcasted_iota(jnp.int32, (NEW, 128), 1)
    for pair in range(HPD // 2):
        two = q_ref[:, 384 * pair : 384 * (pair + 1)].astype(F32)
        for odd in range(2):
            head = 2 * pair + odd
            one = pltpu.roll(two, NOPE + ROPE, 1) if odd else two
            tail = jnp.where(lane < ROPE, one[:, NOPE : NOPE + 128], jnp.where(lane == ROPE, 1.0, 0.0))
            q_out[:, 256 * head : 256 * head + 128] = one[:, :NOPE].astype(BF)
            q_out[:, 256 * head + 128 : 256 * head + 256] = tail.astype(BF)
    rope = jnp.concatenate([lat_ref[KV:, :].astype(F32), jnp.zeros((128 - ROPE, NEW), F32)], 0)
    rope_out[...] = rope.T.astype(BF)
    latent = lat_ref[:KV, :].astype(F32).T.astype(BF)
    kv_out[...] = jnp.dot(latent, w_ref[...], preferred_element_type=F32).astype(BF)


def new_tokens(queries, latent_t, w_ukv):
    return pl.pallas_call(
        new_kernel,
        out_shape=[
            jax.ShapeDtypeStruct((NEW, HPD * 256), BF),
            jax.ShapeDtypeStruct((NEW, HPD * 256), BF),
            jax.ShapeDtypeStruct((NEW, 128), BF),
        ],
        in_specs=[VMEM] * 3,
        out_specs=[VMEM] * 3,
        compiler_params=params(24),
        cost_estimate=cost(2 * NEW * KV * 1024, 4 << 20),
        name="new_tokens",
    )(queries, latent_t, w_ukv)


def turn_kernel(place, w_ref, keep_ref, give_ref, turned):
    width = 2 * SIDE * COLS
    for k in range(width // 256):
        turned[256 * k : 256 * (k + 1), :] = w_ref[:, 256 * k : 256 * (k + 1)].T
    head_id = place[1]
    core = head_id & 1
    x = lax.shift_right_logical(head_id, 1) & (SIDE - 1)
    for d in range(SIDE):
        at = ((x + d) & (SIDE - 1)) * 2
        keep_ref[d, 0] = turned[pl.ds(pl.multiple_of((at + core) * COLS, 32), COLS), :]
        give_ref[d, 0] = turned[pl.ds(pl.multiple_of((at + 1 - core) * COLS, 32), COLS), :]


def turned_weights(place, w_out):
    rows = HPD * VD
    part = jax.ShapeDtypeStruct((SIDE, SIDE, COLS, rows), BF)
    block = pl.BlockSpec((SIDE, 1, COLS, rows), lambda g, s: (0, g, 0, 0))
    return pl.pallas_call(
        turn_kernel,
        out_shape=[part, part],
        grid_spec=pltpu.PrefetchScalarGridSpec(
            num_scalar_prefetch=1,
            grid=(SIDE,),
            in_specs=[
                pl.BlockSpec(
                    (rows, 2 * SIDE * COLS),
                    lambda g, s: (0, (lax.shift_right_logical(s[1], 3) + g) & (SIDE - 1)),
                )
            ],
            out_specs=[block, block],
            scratch_shapes=[pltpu.VMEM((2 * SIDE * COLS, rows), BF)],
        ),
        compiler_params=params(24),
        cost_estimate=cost(0, 24 << 20),
        name="turned_weights",
    )(place, w_out)


def lift_kernel(count, *refs):
    w_ref = refs[count]
    kv_out, rope_out = refs[count + 1 :]
    for i in range(count):
        rows = refs[i].shape[0]
        kv_out[rows * i : rows * (i + 1), :] = jnp.dot(
            refs[i][:, :KV], w_ref[...], preferred_element_type=F32
        ).astype(BF)
        rope_out[rows * i : rows * (i + 1), :] = refs[i][:, KV:]


def lift(pieces, w_ukv):
    count = len(pieces)
    rows = count * pieces[0].shape[0]
    return pl.pallas_call(
        functools.partial(lift_kernel, count),
        out_shape=[
            jax.ShapeDtypeStruct((rows, HPD * 256), BF),
            jax.ShapeDtypeStruct((rows, 128), BF),
        ],
        in_specs=[VMEM] * (count + 1),
        out_specs=[VMEM] * 2,
        compiler_params=params(24),
        cost_estimate=cost(2 * rows * KV * 1024, rows * 4096),
        name="lift",
    )(*pieces, w_ukv)


def attend_kernel(half, groups, q_ref, *refs):
    q = q_ref[...]
    out_ref = refs[-1]
    scores, values = [], []
    for g in range(groups):
        kv = refs[2 * g][...]
        keys = jnp.concatenate([kv[:, :NOPE], refs[2 * g + 1][...]], 1)
        s = lax.dot_general(q, keys, NT, preferred_element_type=F32)
        if g == groups - 1:
            key = lax.broadcasted_iota(jnp.int32, s.shape, 1)
            row = lax.broadcasted_iota(jnp.int32, s.shape, 0) + half * HALF
            s = jnp.where(key <= row, s, BLOCKED)
        scores.append(s)
        values.append(jnp.concatenate([kv[:, NOPE:], jnp.ones((kv.shape[0], 128), BF)], 1))
    top = functools.reduce(jnp.maximum, [jnp.max(s, axis=1, keepdims=True) for s in scores])
    total = None
    for s, v in zip(scores, values):
        weight = jnp.exp2((s - top) * SCALE).astype(BF)
        part = jnp.dot(weight, v, preferred_element_type=F32)
        total = part if total is None else total + part
    out_ref[...] = (total[:, :VD] / total[:, VD:]).astype(BF)


def attend(half, q_ext, prefix, new):
    groups = len(prefix) + 1
    new_rows = HALF * (half + 1)
    specs, operands, keys = [], [], 0
    for kv, rope in prefix + [new]:
        rows = new_rows if kv is new[0] else kv.shape[0]
        keys += rows
        specs += [
            pl.BlockSpec((rows, 256), lambda h: (0, h)),
            pl.BlockSpec((rows, 128), lambda h: (0, 0)),
        ]
        operands += [kv, rope]
    return pl.pallas_call(
        functools.partial(attend_kernel, half, groups),
        out_shape=jax.ShapeDtypeStruct((HALF, HPD * VD), BF),
        grid=(HPD,),
        in_specs=[pl.BlockSpec((HALF, 256), lambda h: (half, h))] + specs,
        out_specs=pl.BlockSpec((HALF, VD), lambda h: (0, h)),
        compiler_params=params(32),
        cost_estimate=cost(HPD * HALF * keys * 1024, keys * 2048, HPD * HALF * keys),
        name="attend",
    )(q_ext, *operands)


def project_kernel(att_ref, other_ref, keep_ref, got_ref, out_ref):
    rows = keep_ref.shape[0] * keep_ref.shape[1] * COLS
    out = lax.dot_general(
        keep_ref[...].reshape(rows, HPD * VD), att_ref[...], NT, preferred_element_type=F32
    ) + lax.dot_general(
        got_ref[...].reshape(rows, HPD * VD), other_ref[...], NT, preferred_element_type=F32
    )
    out_ref[...] = out.reshape(1, rows // COLS, COLS, HALF).astype(BF)


def project(first_x, distances, att, other, keep, got):
    count = len(distances)

    def distance(g):
        if count == 1:
            return distances[0]
        return jnp.where(g == 2, 0, 1 + 2 * g)

    if first_x:
        spec = pl.BlockSpec((1, 2, COLS, HPD * VD), lambda g, k: (distance(g), k, 0, 0))
    else:
        spec = pl.BlockSpec((2, 1, COLS, HPD * VD), lambda g, k: (k, distance(g), 0, 0))
    whole = pl.BlockSpec((HALF, HPD * VD), lambda g, k: (0, 0))
    rows = count * SIDE * COLS
    return pl.pallas_call(
        project_kernel,
        out_shape=jax.ShapeDtypeStruct((count, SIDE, COLS, HALF), BF),
        grid=(count, 2),
        in_specs=[whole, whole, spec, spec],
        out_specs=pl.BlockSpec((1, 2, COLS, HALF), lambda g, k: (g, k, 0, 0)),
        compiler_params=params(16),
        cost_estimate=cost(2 * rows * 1024 * HALF, rows * 2560),
        name="project",
    )(att, other, keep, got)


def add(*terms):
    total = terms[0].astype(F32)
    for term in terms[1:]:
        total = total + term.astype(F32)
    return total.astype(BF)


def summed(first_x, att, other, keep, got):
    one, two = (along_x, along_y) if first_x else (along_y, along_x)
    far = project(first_x, (2,), att, other, keep, got)[0]
    low = send(far[:2], one(1))
    high = send(far[2:], one(-1))
    near = project(first_x, (1, 3, 0), att, other, keep, got)
    up = jnp.concatenate([add(near[0, :2], low), near[0, 2:]], 0)
    down = jnp.concatenate([near[1, :2], add(near[1, 2:], high)], 0)
    part = add(near[2], send(up, one(1)), send(down, one(-1)))
    return add(part[0], send(part[2], two(2)), send(part[1], two(1)), send(part[3], two(-1)))


def per_device(queries, new_latent, latent_pool, w_ukv, w_out, cached_len, page_loc):
    place = jnp.stack([lax.axis_index("pool"), lax.axis_index("head")]).astype(jnp.int32)
    outgoing = own_pages(place, cached_len, page_loc, latent_pool)
    arrived = lax.all_to_all(outgoing, "pool", split_axis=0, concat_axis=0, tiled=True)
    own = arrived.reshape(REQ * PAGE, PAY)
    keep, give = turned_weights(place, w_out)
    got = send(give, SWAP)
    q_ext, kv_new, rope_new = new_tokens(queries, new_latent.T, w_ukv)
    line = jnp.concatenate(
        [own, send(own, along_x(1)), send(own, along_x(-1)), send(own, along_x(2))], 0
    )
    plane = [send(line, along_y(2)), send(line, along_y(1)), send(line, along_y(-1))]
    near = lift([line, send(line, SWAP)], w_ukv)
    far = lift(plane + [send(piece, SWAP) for piece in plane], w_ukv)
    halves = []
    for half in range(2):
        att = attend(half, q_ext, [near, far], (kv_new, rope_new))
        halves.append(summed(half == 0, att, send(att, SWAP), keep, got))
    return jnp.concatenate(halves, 1).T


def solution(mesh):
    placed = (
        P("pool", "head"),
        P("pool", None),
        P(("pool", "head"), None),
        P(None, "head"),
        P("head", None),
        P(),
        P(),
    )
    return jax.shard_map(
        per_device, mesh=mesh, in_specs=placed, out_specs=P("pool", "head"), check_vma=False
    )
```

```python
import functools

import jax
import jax.numpy as jnp
from jax import lax
from jax.experimental import pallas as pl
from jax.experimental.pallas import tpu as pltpu
from jax.sharding import PartitionSpec as P

NOPE = 128
ROPE = 64
VD = 128
KV = 512
NEW = 512
PAGE = 8
MAXP = 256
HPD = 4
REQ = 8
N_HEAD = 32
PAGES_DEV = 16
D = 7168
COLS = D // N_HEAD
WIDTH = KV + ROPE
PAY = KV + 128
HALF = NEW // 2
SIDE = 4
BLOCKED = -1e30
SCALE = (NOPE + ROPE) ** -0.5 * 1.4426950408889634
BF = jnp.bfloat16
F32 = jnp.float32
NT = (((1,), (1,)), ((), ()))
VMEM = pl.BlockSpec(memory_space=pltpu.VMEM)
SMEM = pl.BlockSpec(memory_space=pltpu.SMEM)


PLANE = ("y_hi", "y_lo", "x_hi", "x_lo", "core")


def plane_perm(move):
    def index(y, x, c):
        return ((y % SIDE) * SIDE + x % SIDE) * 2 + c

    return [
        (index(y, x, c), index(*move(y, x, c)))
        for y in range(SIDE)
        for x in range(SIDE)
        for c in range(2)
    ]


SWAP = plane_perm(lambda y, x, c: (y, x, 1 - c))


def send_first(value, d):
    perm = plane_perm(lambda y, x, c: (y + d * c, x + d * (1 - c), c))
    return lax.ppermute(value, PLANE, perm)


def send_second(value, d):
    perm = plane_perm(lambda y, x, c: (y + d * (1 - c), x + d * c, c))
    return lax.ppermute(value, PLANE, perm)


def swap(value):
    return lax.ppermute(value, PLANE, SWAP)


def in_hbm(value):
    return pltpu.with_memory_space_constraint(value, pltpu.HBM)


def params(mib):
    return pltpu.CompilerParams(vmem_limit_bytes=mib << 20)


SHORT = pl.CostEstimate(flops=0, bytes_accessed=1024, transcendentals=0)
LONG = pl.CostEstimate(flops=10**11, bytes_accessed=1024, transcendentals=0)


def pages_kernel(place, lens_in, locs_in, pool_in, out_ref, lens, locs, pool_ref, wide, rows, sems):
    copies = [
        pltpu.make_async_copy(source, target, sems.at[k])
        for k, (source, target) in enumerate([(lens_in, lens), (locs_in, locs), (pool_in, pool_ref)])
    ]
    for copy in copies:
        copy.start()
    for copy in copies:
        copy.wait()
    wide[...] = pool_ref[...].astype(F32)
    pool_id = place[0]
    head_id = place[1]
    lane = lax.broadcasted_iota(jnp.int32, (1, 128), 1)

    def one_request(r, carry):
        sel = jnp.int32(0)
        slot = jnp.int32(0)
        for i in range(MAXP // N_HEAD):
            loc = locs[r, head_id + i * N_HEAD]
            mine = lax.shift_right_logical(loc, 9) == pool_id
            sel = jnp.where(mine, loc & (PAGES_DEV - 1), sel)
            slot = jnp.where(mine, head_id + i * N_HEAD, slot)
        length = lens[r]
        for u in range(PAGE // 2):
            two = wide[pl.ds(sel, 1), 2 * WIDTH * u : 2 * WIDTH * (u + 1)]
            for odd in range(2):
                t = 2 * u + odd
                token = pltpu.roll(two, WIDTH, 1) if odd else two
                extra = jnp.where(slot * PAGE + t < length, 0.0, BLOCKED)
                tail = jnp.where(lane < ROPE, token[:, KV:PAY], jnp.where(lane == ROPE, extra, 0.0))
                rows[r, t : t + 1, :KV] = token[:, :KV]
                rows[r, t : t + 1, KV:] = tail
        return carry

    lax.fori_loop(0, REQ, one_request, 0)
    out_ref[...] = rows[...].astype(BF)


def own_pages(place, cached_len, page_loc, latent_pool):
    return pl.pallas_call(
        pages_kernel,
        out_shape=jax.ShapeDtypeStruct((REQ, PAGE, PAY), BF),
        in_specs=[SMEM] + [pl.BlockSpec(memory_space=pltpu.HBM)] * 3,
        out_specs=VMEM,
        scratch_shapes=[
            pltpu.SMEM((REQ,), jnp.int32),
            pltpu.SMEM((REQ, MAXP), jnp.int32),
            pltpu.VMEM((PAGES_DEV, PAGE * WIDTH), BF),
            pltpu.VMEM((PAGES_DEV, PAGE * WIDTH), F32),
            pltpu.VMEM((REQ, PAGE, PAY), F32),
            pltpu.SemaphoreType.DMA((3,)),
        ],
        compiler_params=params(8),
        cost_estimate=SHORT,
        name="own_pages",
    )(place, in_hbm(cached_len), in_hbm(page_loc), in_hbm(latent_pool))


def new_kernel(q_ref, lat_ref, w_ref, q_out, kv_out, rope_out):
    lane = lax.broadcasted_iota(jnp.int32, (NEW, 128), 1)
    for pair in range(HPD // 2):
        two = q_ref[:, 384 * pair : 384 * (pair + 1)].astype(F32)
        for odd in range(2):
            head = 2 * pair + odd
            one = pltpu.roll(two, NOPE + ROPE, 1) if odd else two
            tail = jnp.where(lane < ROPE, one[:, NOPE : NOPE + 128], jnp.where(lane == ROPE, 1.0, 0.0))
            q_out[:, 256 * head : 256 * head + 128] = one[:, :NOPE].astype(BF)
            q_out[:, 256 * head + 128 : 256 * head + 256] = tail.astype(BF)
    rope = jnp.concatenate([lat_ref[KV:, :].astype(F32), jnp.zeros((128 - ROPE, NEW), F32)], 0)
    rope_out[...] = rope.T.astype(BF)
    latent = lat_ref[:KV, :].astype(F32).T.astype(BF)
    kv_out[...] = jnp.dot(latent, w_ref[...], preferred_element_type=F32).astype(BF)


def new_tokens(queries, latent_t, w_ukv):
    return pl.pallas_call(
        new_kernel,
        out_shape=[
            jax.ShapeDtypeStruct((NEW, HPD * 256), BF),
            jax.ShapeDtypeStruct((NEW, HPD * 256), BF),
            jax.ShapeDtypeStruct((NEW, 128), BF),
        ],
        in_specs=[VMEM] * 3,
        out_specs=[VMEM] * 3,
        compiler_params=params(24),
        cost_estimate=SHORT,
        name="new_tokens",
    )(in_hbm(queries), in_hbm(latent_t), w_ukv)


def turn_kernel(place, w_ref, keep_ref, give_ref, flag_ref, turned):
    flag_ref[...] = jnp.zeros_like(flag_ref)
    width = 2 * SIDE * COLS
    for k in range(width // 256):
        turned[256 * k : 256 * (k + 1), :] = w_ref[:, 256 * k : 256 * (k + 1)].T
    head_id = place[1]
    core = head_id & 1
    x = lax.shift_right_logical(head_id, 1) & (SIDE - 1)
    dy = pl.program_id(0)
    for dx in range(SIDE):
        at = ((x + dx) & (SIDE - 1)) * 2
        mine = (jnp.where(core == 0, dx, dy), jnp.where(core == 0, dy + 3, dx + 3) & (SIDE - 1))
        theirs = (jnp.where(core == 0, dy, dx), jnp.where(core == 0, dx + 3, dy + 3) & (SIDE - 1))
        keep_ref[mine] = turned[pl.ds(pl.multiple_of((at + core) * COLS, 32), COLS), :]
        give_ref[theirs] = turned[pl.ds(pl.multiple_of((at + 1 - core) * COLS, 32), COLS), :]


def turned_weights(place, w_out):
    rows = HPD * VD
    part = jax.ShapeDtypeStruct((SIDE, SIDE, COLS, rows), BF)
    whole = pl.BlockSpec((SIDE, SIDE, COLS, rows), lambda g, s: (0, 0, 0, 0))

    def column(g, s):
        return (0, (lax.shift_right_logical(s[1], 3) + g) & (SIDE - 1))

    return pl.pallas_call(
        turn_kernel,
        out_shape=[part, part, jax.ShapeDtypeStruct((8, 128), F32)],
        grid_spec=pltpu.PrefetchScalarGridSpec(
            num_scalar_prefetch=1,
            grid=(SIDE,),
            in_specs=[pl.BlockSpec((rows, 2 * SIDE * COLS), column)],
            out_specs=[whole, whole, pl.BlockSpec((8, 128), lambda g, s: (0, 0))],
            scratch_shapes=[pltpu.VMEM((2 * SIDE * COLS, rows), BF)],
        ),
        compiler_params=params(28),
        cost_estimate=SHORT,
        name="turned_weights",
    )(place, in_hbm(w_out))


def lift_kernel(count, *refs):
    w_ref = refs[count]
    kv_out, rope_out = refs[count + 1 :]
    for i in range(count):
        rows = refs[i].shape[0]
        kv_out[rows * i : rows * (i + 1), :] = jnp.dot(
            refs[i][:, :KV], w_ref[...], preferred_element_type=F32
        ).astype(BF)
        rope_out[rows * i : rows * (i + 1), :] = refs[i][:, KV:]


def lift(pieces, w_ukv):
    count = len(pieces)
    rows = count * pieces[0].shape[0]
    return pl.pallas_call(
        functools.partial(lift_kernel, count),
        out_shape=[
            jax.ShapeDtypeStruct((rows, HPD * 256), BF),
            jax.ShapeDtypeStruct((rows, 128), BF),
        ],
        in_specs=[VMEM] * (count + 1),
        out_specs=[VMEM] * 2,
        compiler_params=params(24),
        cost_estimate=SHORT,
        name="lift",
    )(*pieces, w_ukv)


def group_scores(q, kv, rope):
    keys = jnp.concatenate([kv[:, :NOPE], rope], 1)
    return lax.dot_general(q, keys, NT, preferred_element_type=F32)


def group_sum(weight, kv):
    values = jnp.concatenate([kv[:, NOPE:], jnp.ones((kv.shape[0], 128), BF)], 1)
    return jnp.dot(weight, values, preferred_element_type=F32)


LARGE = 2.0**60


def weights_of(s, top):
    return jnp.exp2((s - top) * SCALE).astype(BF)


def row_max(s):
    return jnp.max(s, axis=1, keepdims=True)


def new_scores(half, q, kv_new, rope_new):
    count = HALF * (half + 1)
    n = group_scores(q, kv_new[:count, :], rope_new[:count, :])
    key = lax.broadcasted_iota(jnp.int32, n.shape, 1)
    row = lax.broadcasted_iota(jnp.int32, n.shape, 0) + half * HALF
    return jnp.where(key <= row, n, BLOCKED)


def near_kernel(q_ref, kv_ref, rope_ref, kv_new, rope_new, sum_ref, top_ref):
    def work(exact):
        for half in range(2):
            rows = slice(half * HALF, (half + 1) * HALF)
            count = HALF * (half + 1)
            q = q_ref[rows, :]
            n = new_scores(half, q, kv_new, rope_new)
            top = row_max(n)
            s = group_scores(q, kv_ref[...], rope_ref[...])
            if exact:
                top = jnp.maximum(top, row_max(s))
            sum_ref[rows, :] = group_sum(weights_of(s, top), kv_ref[...]) + group_sum(
                weights_of(n, top), kv_new[:count, :]
            )
            top_ref[rows, :] = jnp.broadcast_to(top, (HALF, 128))

    work(False)
    fine = jnp.max(sum_ref[:, VD:]) < LARGE

    @pl.when(jnp.logical_not(fine))
    def _():
        work(True)


def attend_near(q_ext, kv, rope, kv_new, rope_new):
    head = pl.BlockSpec((NEW, 256), lambda h: (0, h))
    whole = pl.BlockSpec((NEW, 128), lambda h: (0, 0))
    return pl.pallas_call(
        near_kernel,
        out_shape=[
            jax.ShapeDtypeStruct((NEW, HPD * 256), F32),
            jax.ShapeDtypeStruct((NEW, HPD * 128), F32),
        ],
        grid=(HPD,),
        in_specs=[head, head, whole, head, whole],
        out_specs=[head, pl.BlockSpec((NEW, 128), lambda h: (0, h))],
        compiler_params=params(16),
        cost_estimate=SHORT,
        name="attend_near",
    )(q_ext, kv, rope, kv_new, rope_new)


def far_kernel(groups, q_ref, sum_ref, top_ref, order_ref, *refs):
    out_ref, total_ref = refs[-2:]
    old = top_ref[:, :1]

    def work(exact):
        q = q_ref[...]
        scores = [group_scores(q, refs[2 * g][...], refs[2 * g + 1][...]) for g in range(groups)]
        total = sum_ref[...]
        top = old
        if exact:
            top = functools.reduce(jnp.maximum, [row_max(s) for s in scores] + [old])
            total = total * jnp.exp2((old - top) * SCALE)
        for g, s in enumerate(scores):
            total = total + group_sum(weights_of(s, top), refs[2 * g][...])
        total_ref[...] = total

    work(False)
    fine = jnp.max(total_ref[:, VD:]) < LARGE

    @pl.when(jnp.logical_not(fine))
    def _():
        work(True)

    out_ref[...] = (total_ref[:, :VD] / total_ref[:, VD:]).astype(BF)


def attend_far(q_ext, sums, tops, order, far):
    specs, operands, keys = [], [], 0
    for kv, rope in far:
        rows = kv.shape[0]
        keys += rows
        specs += [
            pl.BlockSpec((rows, 256), lambda h: (0, h)),
            pl.BlockSpec((rows, 128), lambda h: (0, 0)),
        ]
        operands += [kv, rope]
    head = pl.BlockSpec((NEW, 256), lambda h: (0, h))
    return pl.pallas_call(
        functools.partial(far_kernel, len(far)),
        out_shape=jax.ShapeDtypeStruct((NEW, HPD * VD), BF),
        grid=(HPD,),
        in_specs=[head, head, pl.BlockSpec((NEW, 128), lambda h: (0, h)), pl.BlockSpec((8, 128), lambda h: (0, 0))] + specs,
        out_specs=pl.BlockSpec((NEW, VD), lambda h: (0, h)),
        scratch_shapes=[pltpu.VMEM((NEW, 256), F32)],
        compiler_params=params(20),
        cost_estimate=LONG,
        name="attend_far",
    )(q_ext, sums, tops, order, *operands)


def project_kernel(att_ref, other_ref, keep_ref, got_ref, out_ref):
    rows = 2 * COLS
    out = lax.dot_general(
        keep_ref[...].reshape(rows, HPD * VD), att_ref[...], NT, preferred_element_type=F32
    ) + lax.dot_general(
        got_ref[...].reshape(rows, HPD * VD), other_ref[...], NT, preferred_element_type=F32
    )
    out_ref[...] = out.reshape(2, COLS, NEW).astype(BF)


def project(a, pair, att, other, keep, got):
    spec = pl.BlockSpec((1, 2, COLS, HPD * VD), lambda i: (a, pair, 0, 0))
    whole = pl.BlockSpec((NEW, HPD * VD), lambda i: (0, 0))
    rows = 2 * COLS
    return pl.pallas_call(
        project_kernel,
        out_shape=jax.ShapeDtypeStruct((2, COLS, NEW), BF),
        grid=(1,),
        in_specs=[whole, whole, spec, spec],
        out_specs=pl.BlockSpec((2, COLS, NEW), lambda i: (0, 0, 0)),
        compiler_params=params(16),
        cost_estimate=SHORT,
        name="project",
    )(att, other, keep, got)


def add(*terms):
    total = terms[0].astype(F32)
    for term in terms[1:]:
        total = total + term.astype(F32)
    return total.astype(BF)


def per_device(queries, new_latent, latent_pool, w_ukv, w_out, cached_len, page_loc):
    place = jnp.stack([lax.axis_index("pool"), lax.axis_index(PLANE)]).astype(jnp.int32)
    outgoing = own_pages(place, cached_len, page_loc, latent_pool)
    arrived = lax.all_to_all(outgoing, "pool", split_axis=0, concat_axis=0, tiled=True)
    own = arrived.reshape(REQ * PAGE, PAY)
    own, new_latent = lax.optimization_barrier((own, new_latent))
    q_ext, kv_new, rope_new = new_tokens(queries, new_latent.T, w_ukv)
    line = [own, send_first(own, 2), send_first(own, 1), send_first(own, -1)]
    *line, kv_new = lax.optimization_barrier((*line, kv_new))
    line, place = lax.optimization_barrier((jnp.concatenate(line, 0), place))
    pieces = [send_second(line, d) for d in (2, 1, -1)]
    near = lift([line, swap(line)], w_ukv)
    sums, tops = attend_near(q_ext, *near, kv_new, rope_new)
    keep, give, order = turned_weights(place, w_out)
    got = swap(give)
    *pieces, sums, order = lax.optimization_barrier((*pieces, sums, order))
    far = [lift(pieces, w_ukv), lift([swap(piece) for piece in pieces], w_ukv)]
    att = attend_far(q_ext, sums, tops, order, far)
    other = swap(att)
    sent = [
        [send_first(project(a, pair, att, other, keep, got), d) for a, d in ((2, 2), (1, 1), (3, -1))]
        for pair in range(2)
    ]
    one = add(project(0, 0, att, other, keep, got), *sent[0])
    one = [send_second(one[1], 2), send_second(one[0], 1)]
    *sent[1], one[0], one[1] = lax.optimization_barrier((*sent[1], *one))
    two = add(project(0, 1, att, other, keep, got), *sent[1])
    out = add(two[1], *one, send_second(two[0], -1))
    return out.T


def solution(mesh):
    fine = jax.sharding.Mesh(
        mesh.devices.reshape(mesh.shape["pool"], 2, 2, 2, 2, 2), ("pool",) + PLANE
    )
    placed = (
        P("pool", PLANE),
        P("pool", None),
        P(("pool",) + PLANE, None),
        P(None, PLANE),
        P(PLANE, None),
        P(),
        P(),
    )
    return jax.shard_map(
        per_device, mesh=fine, in_specs=placed, out_specs=P("pool", PLANE), check_vma=False
    )
```

```python
import functools

import jax
import jax.numpy as jnp
from jax import lax
from jax.experimental import pallas as pl
from jax.experimental.pallas import tpu as pltpu
from jax.sharding import PartitionSpec as P

NOPE = 128
ROPE = 64
VD = 128
KV = 512
NEW = 512
PAGE = 8
MAXP = 256
HPD = 4
REQ = 8
N_HEAD = 32
PAGES_DEV = 16
D = 7168
COLS = D // N_HEAD
WIDTH = KV + ROPE
PAY = KV + 128
HALF = NEW // 2
SIDE = 4
BLOCKED = -1e30
SCALE = (NOPE + ROPE) ** -0.5 * 1.4426950408889634
BF = jnp.bfloat16
F32 = jnp.float32
NT = (((1,), (1,)), ((), ()))
VMEM = pl.BlockSpec(memory_space=pltpu.VMEM)
SMEM = pl.BlockSpec(memory_space=pltpu.SMEM)


PLANE = ("y_hi", "y_lo", "x_hi", "x_lo", "core")


def plane_perm(move):
    def index(y, x, c):
        return ((y % SIDE) * SIDE + x % SIDE) * 2 + c

    return [
        (index(y, x, c), index(*move(y, x, c)))
        for y in range(SIDE)
        for x in range(SIDE)
        for c in range(2)
    ]


SWAP = plane_perm(lambda y, x, c: (y, x, 1 - c))


def send_first(value, d):
    perm = plane_perm(lambda y, x, c: (y + d * c, x + d * (1 - c), c))
    return lax.ppermute(value, PLANE, perm)


def send_second(value, d):
    perm = plane_perm(lambda y, x, c: (y + d * (1 - c), x + d * c, c))
    return lax.ppermute(value, PLANE, perm)


def swap(value):
    return lax.ppermute(value, PLANE, SWAP)


def in_hbm(value):
    return pltpu.with_memory_space_constraint(value, pltpu.HBM)


def params(mib):
    return pltpu.CompilerParams(vmem_limit_bytes=mib << 20)


SHORT = pl.CostEstimate(flops=0, bytes_accessed=1024, transcendentals=0)
LONG = pl.CostEstimate(flops=10**11, bytes_accessed=1024, transcendentals=0)


def pages_kernel(place, lens_in, locs_in, pool_in, out_ref, lens, locs, pool_ref, wide, chosen, rows, sems):
    copies = [
        pltpu.make_async_copy(source, target, sems.at[k])
        for k, (source, target) in enumerate([(lens_in, lens), (locs_in, locs), (pool_in, pool_ref)])
    ]
    for copy in copies:
        copy.start()
    copies[0].wait()
    copies[1].wait()
    pool_id = place[0]
    head_id = place[1]
    request = lax.broadcasted_iota(jnp.int32, (REQ, 128), 0)
    lane = lax.broadcasted_iota(jnp.int32, (REQ, 128), 1)
    past = jnp.zeros((REQ, 128), jnp.int32)
    picks = []
    for r in range(REQ):
        sel = jnp.int32(0)
        slot = jnp.int32(0)
        for i in range(MAXP // N_HEAD):
            loc = locs[r, head_id + i * N_HEAD]
            mine = lax.shift_right_logical(loc, 9) == pool_id
            sel = jnp.where(mine, loc & (PAGES_DEV - 1), sel)
            slot = jnp.where(mine, head_id + i * N_HEAD, slot)
        picks.append(sel)
        past = jnp.where(request == r, slot * PAGE - lens[r], past)
    copies[2].wait()
    wide[...] = pool_ref[...].astype(F32)
    for r in range(REQ):
        chosen[r : r + 1, :] = wide[pl.ds(picks[r], 1), :]
    for u in range(PAGE // 2):
        two = chosen[:, 2 * WIDTH * u : 2 * WIDTH * (u + 1)]
        for odd in range(2):
            t = 2 * u + odd
            token = pltpu.roll(two, WIDTH, 1) if odd else two
            extra = jnp.where(past + t < 0, 0.0, BLOCKED)
            tail = jnp.where(lane < ROPE, token[:, KV:PAY], jnp.where(lane == ROPE, extra, 0.0))
            for k in range(PAY // 128):
                part = token[:, 128 * k : 128 * (k + 1)] if 128 * k < KV else tail
                rows[k, pl.ds(t, REQ, stride=PAGE), :] = part
    for k in range(PAY // 128):
        out_ref[:, :, 128 * k : 128 * (k + 1)] = rows[k].reshape(REQ, PAGE, 128).astype(BF)


def own_pages(place, cached_len, page_loc, latent_pool):
    return pl.pallas_call(
        pages_kernel,
        out_shape=jax.ShapeDtypeStruct((REQ, PAGE, PAY), BF),
        in_specs=[SMEM] + [pl.BlockSpec(memory_space=pltpu.HBM)] * 3,
        out_specs=VMEM,
        scratch_shapes=[
            pltpu.SMEM((REQ,), jnp.int32),
            pltpu.SMEM((REQ, MAXP), jnp.int32),
            pltpu.VMEM((PAGES_DEV, PAGE * WIDTH), BF),
            pltpu.VMEM((PAGES_DEV, PAGE * WIDTH), F32),
            pltpu.VMEM((REQ, PAGE * WIDTH), F32),
            pltpu.VMEM((PAY // 128, REQ * PAGE, 128), F32),
            pltpu.SemaphoreType.DMA((3,)),
        ],
        compiler_params=params(8),
        cost_estimate=SHORT,
        name="own_pages",
    )(place, in_hbm(cached_len), in_hbm(page_loc), in_hbm(latent_pool))


def new_kernel(q_ref, lat_ref, w_ref, q_out, kv_out, rope_out):
    lane = lax.broadcasted_iota(jnp.int32, (NEW, 128), 1)
    for pair in range(HPD // 2):
        two = q_ref[:, 384 * pair : 384 * (pair + 1)].astype(F32)
        for odd in range(2):
            head = 2 * pair + odd
            one = pltpu.roll(two, NOPE + ROPE, 1) if odd else two
            tail = jnp.where(lane < ROPE, one[:, NOPE : NOPE + 128], jnp.where(lane == ROPE, 1.0, 0.0))
            q_out[:, 256 * head : 256 * head + 128] = one[:, :NOPE].astype(BF)
            q_out[:, 256 * head + 128 : 256 * head + 256] = tail.astype(BF)
    rope = jnp.concatenate([lat_ref[KV:, :].astype(F32), jnp.zeros((128 - ROPE, NEW), F32)], 0)
    rope_out[...] = rope.T.astype(BF)
    latent = lat_ref[:KV, :].astype(F32).T.astype(BF)
    kv_out[...] = jnp.dot(latent, w_ref[...], preferred_element_type=F32).astype(BF)


def new_tokens(queries, latent_t, w_ukv):
    return pl.pallas_call(
        new_kernel,
        out_shape=[
            jax.ShapeDtypeStruct((NEW, HPD * 256), BF),
            jax.ShapeDtypeStruct((NEW, HPD * 256), BF),
            jax.ShapeDtypeStruct((NEW, 128), BF),
        ],
        in_specs=[VMEM] * 3,
        out_specs=[VMEM] * 3,
        compiler_params=params(24),
        cost_estimate=SHORT,
        name="new_tokens",
    )(in_hbm(queries), in_hbm(latent_t), w_ukv)


def lift_kernel(count, *refs):
    w_ref = refs[count]
    kv_out, rope_out = refs[count + 1 :]
    for i in range(count):
        rows = refs[i].shape[0]
        kv_out[rows * i : rows * (i + 1), :] = jnp.dot(
            refs[i][:, :KV], w_ref[...], preferred_element_type=F32
        ).astype(BF)
        rope_out[rows * i : rows * (i + 1), :] = refs[i][:, KV:]


def lift(pieces, w_ukv):
    count = len(pieces)
    rows = count * pieces[0].shape[0]
    return pl.pallas_call(
        functools.partial(lift_kernel, count),
        out_shape=[
            jax.ShapeDtypeStruct((rows, HPD * 256), BF),
            jax.ShapeDtypeStruct((rows, 128), BF),
        ],
        in_specs=[VMEM] * (count + 1),
        out_specs=[VMEM] * 2,
        compiler_params=params(24),
        cost_estimate=SHORT,
        name="lift",
    )(*pieces, w_ukv)


def group_scores(q, kv, rope):
    keys = jnp.concatenate([kv[:, :NOPE], rope], 1)
    return lax.dot_general(q, keys, NT, preferred_element_type=F32)


def group_sum(weight, kv):
    values = jnp.concatenate([kv[:, NOPE:], jnp.ones((kv.shape[0], 128), BF)], 1)
    return jnp.dot(weight, values, preferred_element_type=F32)


LARGE = 2.0**60


def weights_of(s, top):
    return jnp.exp2((s - top) * SCALE).astype(BF)


def row_max(s):
    return jnp.max(s, axis=1, keepdims=True)


def new_scores(half, q, kv_new, rope_new):
    count = HALF * (half + 1)
    n = group_scores(q, kv_new[:count, :], rope_new[:count, :])
    key = lax.broadcasted_iota(jnp.int32, n.shape, 1)
    row = lax.broadcasted_iota(jnp.int32, n.shape, 0) + half * HALF
    return jnp.where(key <= row, n, BLOCKED)


def near_kernel(
    place, q_ref, kv_ref, rope_ref, kv_new, rope_new, w_ref, sum_ref, top_ref, keep_ref, give_ref, turned
):
    def work(exact):
        for half in range(2):
            rows = slice(half * HALF, (half + 1) * HALF)
            count = HALF * (half + 1)
            q = q_ref[rows, :]
            n = new_scores(half, q, kv_new, rope_new)
            top = row_max(n)
            s = group_scores(q, kv_ref[...], rope_ref[...])
            if exact:
                top = jnp.maximum(top, row_max(s))
            sum_ref[rows, :] = group_sum(weights_of(s, top), kv_ref[...]) + group_sum(
                weights_of(n, top), kv_new[:count, :]
            )
            top_ref[rows, :] = jnp.broadcast_to(top, (HALF, 128))

    for k in range(2 * SIDE * COLS // 256):
        turned[256 * k : 256 * (k + 1), :] = w_ref[:, 256 * k : 256 * (k + 1)].T
    work(False)
    head_id = place[1]
    core = head_id & 1
    x = lax.shift_right_logical(head_id, 1) & (SIDE - 1)
    dy = pl.program_id(0)
    for dx in range(SIDE):
        at = ((x + dx) & (SIDE - 1)) * 2
        mine = (jnp.where(core == 0, dx, dy), jnp.where(core == 0, dy + 3, dx + 3) & (SIDE - 1))
        theirs = (jnp.where(core == 0, dy, dx), jnp.where(core == 0, dx + 3, dy + 3) & (SIDE - 1))
        keep_ref[mine] = turned[pl.ds(pl.multiple_of((at + core) * COLS, 32), COLS), :]
        give_ref[theirs] = turned[pl.ds(pl.multiple_of((at + 1 - core) * COLS, 32), COLS), :]
    fine = jnp.max(sum_ref[:, VD:]) < LARGE

    @pl.when(jnp.logical_not(fine))
    def _():
        work(True)


def attend_near(place, q_ext, kv, rope, kv_new, rope_new, w_out):
    head = pl.BlockSpec((NEW, 256), lambda h, s: (0, h))
    rope_spec = pl.BlockSpec((NEW, 128), lambda h, s: (0, 0))
    rows = HPD * VD
    part = jax.ShapeDtypeStruct((SIDE, SIDE, COLS, rows), BF)
    whole = pl.BlockSpec((SIDE, SIDE, COLS, rows), lambda h, s: (0, 0, 0, 0))

    def column(h, s):
        return (0, (lax.shift_right_logical(s[1], 3) + h) & (SIDE - 1))

    return pl.pallas_call(
        near_kernel,
        out_shape=[
            jax.ShapeDtypeStruct((NEW, HPD * 256), F32),
            jax.ShapeDtypeStruct((NEW, HPD * 128), F32),
            part,
            part,
        ],
        grid_spec=pltpu.PrefetchScalarGridSpec(
            num_scalar_prefetch=1,
            grid=(HPD,),
            in_specs=[head, head, rope_spec, head, rope_spec, pl.BlockSpec((rows, 2 * SIDE * COLS), column)],
            out_specs=[head, pl.BlockSpec((NEW, 128), lambda h, s: (0, h)), whole, whole],
            scratch_shapes=[pltpu.VMEM((2 * SIDE * COLS, rows), BF)],
        ),
        compiler_params=params(36),
        cost_estimate=SHORT,
        name="attend_near",
    )(place, q_ext, kv, rope, kv_new, rope_new, in_hbm(w_out))


def far_kernel(groups, q_ref, sum_ref, top_ref, *refs):
    out_ref, total_ref = refs[-2:]
    old = top_ref[:, :1]

    def work(exact):
        q = q_ref[...]
        scores = [group_scores(q, refs[2 * g][...], refs[2 * g + 1][...]) for g in range(groups)]
        total = sum_ref[...]
        top = old
        if exact:
            top = functools.reduce(jnp.maximum, [row_max(s) for s in scores] + [old])
            total = total * jnp.exp2((old - top) * SCALE)
        for g, s in enumerate(scores):
            total = total + group_sum(weights_of(s, top), refs[2 * g][...])
        total_ref[...] = total

    work(False)
    fine = jnp.max(total_ref[:, VD:]) < LARGE

    @pl.when(jnp.logical_not(fine))
    def _():
        work(True)

    out_ref[...] = (total_ref[:, :VD] / total_ref[:, VD:]).astype(BF)


def attend_far(q_ext, sums, tops, far):
    specs, operands, keys = [], [], 0
    for kv, rope in far:
        rows = kv.shape[0]
        keys += rows
        specs += [
            pl.BlockSpec((rows, 256), lambda h: (0, h)),
            pl.BlockSpec((rows, 128), lambda h: (0, 0)),
        ]
        operands += [kv, rope]
    head = pl.BlockSpec((NEW, 256), lambda h: (0, h))
    return pl.pallas_call(
        functools.partial(far_kernel, len(far)),
        out_shape=jax.ShapeDtypeStruct((NEW, HPD * VD), BF),
        grid=(HPD,),
        in_specs=[head, head, pl.BlockSpec((NEW, 128), lambda h: (0, h))] + specs,
        out_specs=pl.BlockSpec((NEW, VD), lambda h: (0, h)),
        scratch_shapes=[pltpu.VMEM((NEW, 256), F32)],
        compiler_params=params(20),
        cost_estimate=LONG,
        name="attend_far",
    )(q_ext, sums, tops, *operands)


def project_kernel(att_ref, other_ref, keep_ref, got_ref, out_ref):
    rows = out_ref.shape[0] * COLS
    out = lax.dot_general(
        keep_ref[...].reshape(rows, HPD * VD), att_ref[...], NT, preferred_element_type=F32
    ) + lax.dot_general(
        got_ref[...].reshape(rows, HPD * VD), other_ref[...], NT, preferred_element_type=F32
    )
    out_ref[...] = out.reshape(out_ref.shape).astype(BF)


def project(a, first, count, att, other, keep, got):
    spec = pl.BlockSpec((1, count, COLS, HPD * VD), lambda i: (a, first // count, 0, 0))
    whole = pl.BlockSpec((NEW, HPD * VD), lambda i: (0, 0))
    return pl.pallas_call(
        project_kernel,
        out_shape=jax.ShapeDtypeStruct((count, COLS, NEW), BF),
        grid=(1,),
        in_specs=[whole, whole, spec, spec],
        out_specs=pl.BlockSpec((count, COLS, NEW), lambda i: (0, 0, 0)),
        compiler_params=params(16),
        cost_estimate=SHORT,
        name="project",
    )(att, other, keep, got)


def add(*terms):
    total = terms[0].astype(F32)
    for term in terms[1:]:
        total = total + term.astype(F32)
    return total.astype(BF)


def per_device(queries, new_latent, latent_pool, w_ukv, w_out, cached_len, page_loc):
    place = jnp.stack([lax.axis_index("pool"), lax.axis_index(PLANE)]).astype(jnp.int32)
    outgoing = own_pages(place, cached_len, page_loc, latent_pool)
    arrived = lax.all_to_all(outgoing, "pool", split_axis=0, concat_axis=0, tiled=True)
    own = arrived.reshape(REQ * PAGE, PAY)
    own, new_latent = lax.optimization_barrier((own, new_latent))
    q_ext, kv_new, rope_new = new_tokens(queries, new_latent.T, w_ukv)
    line = [own, send_first(own, 2), send_first(own, 1), send_first(own, -1)]
    *line, kv_new = lax.optimization_barrier((*line, kv_new))
    line = jnp.concatenate(line, 0)
    pieces = [send_second(line, d) for d in (2, 1, -1)]
    near = lift([line, swap(line)], w_ukv)
    sums, tops, keep, give = attend_near(place, q_ext, *near, kv_new, rope_new, w_out)
    got = swap(give)
    *pieces, sums = lax.optimization_barrier((*pieces, sums))
    far = [lift(pieces, w_ukv), lift([swap(piece) for piece in pieces], w_ukv)]
    att = attend_far(q_ext, sums, tops, far)
    other = swap(att)
    def partial_sums(a, half):
        return project(a, 2 * half, 2, att, other, keep, got)

    far_parts = [partial_sums(2, half) for half in range(2)]
    att, far_parts[1] = lax.optimization_barrier((att, far_parts[1]))
    passing = send_first(far_parts[0], 1), send_first(far_parts[1], -1)
    early = send_first(partial_sums(1, 1), 1), send_first(partial_sums(3, 0), -1)
    late = (
        send_first(add(partial_sums(1, 0), passing[0]), 1),
        send_first(add(partial_sums(3, 1), passing[1]), -1),
    )
    one, two = add(partial_sums(0, 0), late[0], early[1])
    rest = partial_sums(0, 1), early[0], late[1]
    three = add(*[value[0] for value in rest])
    moved = [send_second(two, 2), send_second(one, 1), send_second(three, -1)]
    out = add(*[value[1] for value in rest], *moved)
    return out.T


def solution(mesh):
    fine = jax.sharding.Mesh(
        mesh.devices.reshape(mesh.shape["pool"], 2, 2, 2, 2, 2), ("pool",) + PLANE
    )
    placed = (
        P("pool", PLANE),
        P("pool", None),
        P(("pool",) + PLANE, None),
        P(None, PLANE),
        P(PLANE, None),
        P(),
        P(),
    )
    return jax.shard_map(
        per_device, mesh=fine, in_specs=placed, out_specs=P("pool", PLANE), check_vma=False
    )
```

```python
import functools

import jax
import jax.numpy as jnp
from jax import lax
from jax.experimental import pallas as pl
from jax.experimental.pallas import tpu as pltpu
from jax.sharding import PartitionSpec as P

NOPE = 128
ROPE = 64
VD = 128
KV = 512
NEW = 512
PAGE = 8
MAXP = 256
HPD = 4
REQ = 8
N_HEAD = 32
PAGES_DEV = 16
D = 7168
COLS = D // N_HEAD
WIDTH = KV + ROPE
PAY = KV + 128
HALF = NEW // 2
SIDE = 4
BLOCKED = -1e30
SCALE = (NOPE + ROPE) ** -0.5 * 1.4426950408889634
BF = jnp.bfloat16
F32 = jnp.float32
NT = (((1,), (1,)), ((), ()))
VMEM = pl.BlockSpec(memory_space=pltpu.VMEM)
SMEM = pl.BlockSpec(memory_space=pltpu.SMEM)


PLANE = ("y_hi", "y_lo", "x_hi", "x_lo", "core")


def plane_perm(move):
    def index(y, x, c):
        return ((y % SIDE) * SIDE + x % SIDE) * 2 + c

    return [
        (index(y, x, c), index(*move(y, x, c)))
        for y in range(SIDE)
        for x in range(SIDE)
        for c in range(2)
    ]


SWAP = plane_perm(lambda y, x, c: (y, x, 1 - c))


def send_first(value, d):
    perm = plane_perm(lambda y, x, c: (y + d * c, x + d * (1 - c), c))
    return lax.ppermute(value, PLANE, perm)


def send_second(value, d):
    perm = plane_perm(lambda y, x, c: (y + d * (1 - c), x + d * c, c))
    return lax.ppermute(value, PLANE, perm)


def swap(value):
    return lax.ppermute(value, PLANE, SWAP)


def in_hbm(value):
    return pltpu.with_memory_space_constraint(value, pltpu.HBM)


def params(mib):
    return pltpu.CompilerParams(vmem_limit_bytes=mib << 20)


SHORT = pl.CostEstimate(flops=0, bytes_accessed=1024, transcendentals=0)
LONG = pl.CostEstimate(flops=10**11, bytes_accessed=1024, transcendentals=0)


def pages_kernel(place, lens_in, locs_in, pool_in, out_ref, lens, locs, pool_ref, wide, chosen, rows, sems):
    copies = [
        pltpu.make_async_copy(source, target, sems.at[k])
        for k, (source, target) in enumerate([(lens_in, lens), (locs_in, locs), (pool_in, pool_ref)])
    ]
    for copy in copies:
        copy.start()
    copies[0].wait()
    copies[1].wait()
    pool_id = place[0]
    head_id = place[1]
    request = lax.broadcasted_iota(jnp.int32, (REQ, 128), 0)
    lane = lax.broadcasted_iota(jnp.int32, (REQ, 128), 1)
    past = jnp.zeros((REQ, 128), jnp.int32)
    picks = []
    for r in range(REQ):
        sel = jnp.int32(0)
        slot = jnp.int32(0)
        for i in range(MAXP // N_HEAD):
            loc = locs[r, head_id + i * N_HEAD]
            mine = lax.shift_right_logical(loc, 9) == pool_id
            sel = jnp.where(mine, loc & (PAGES_DEV - 1), sel)
            slot = jnp.where(mine, head_id + i * N_HEAD, slot)
        picks.append(sel)
        past = jnp.where(request == r, slot * PAGE - lens[r], past)
    copies[2].wait()
    wide[...] = pool_ref[...].astype(F32)
    for r in range(REQ):
        chosen[r : r + 1, :] = wide[pl.ds(picks[r], 1), :]
    for u in range(PAGE // 2):
        two = chosen[:, 2 * WIDTH * u : 2 * WIDTH * (u + 1)]
        for odd in range(2):
            t = 2 * u + odd
            token = pltpu.roll(two, WIDTH, 1) if odd else two
            extra = jnp.where(past + t < 0, 0.0, BLOCKED)
            tail = jnp.where(lane < ROPE, token[:, KV:PAY], jnp.where(lane == ROPE, extra, 0.0))
            for k in range(PAY // 128):
                part = token[:, 128 * k : 128 * (k + 1)] if 128 * k < KV else tail
                rows[k, pl.ds(t, REQ, stride=PAGE), :] = part
    for k in range(PAY // 128):
        out_ref[:, :, 128 * k : 128 * (k + 1)] = rows[k].reshape(REQ, PAGE, 128).astype(BF)


def own_pages(place, cached_len, page_loc, latent_pool):
    return pl.pallas_call(
        pages_kernel,
        out_shape=jax.ShapeDtypeStruct((REQ, PAGE, PAY), BF),
        in_specs=[SMEM] + [pl.BlockSpec(memory_space=pltpu.HBM)] * 3,
        out_specs=VMEM,
        scratch_shapes=[
            pltpu.SMEM((REQ,), jnp.int32),
            pltpu.SMEM((REQ, MAXP), jnp.int32),
            pltpu.VMEM((PAGES_DEV, PAGE * WIDTH), BF),
            pltpu.VMEM((PAGES_DEV, PAGE * WIDTH), F32),
            pltpu.VMEM((REQ, PAGE * WIDTH), F32),
            pltpu.VMEM((PAY // 128, REQ * PAGE, 128), F32),
            pltpu.SemaphoreType.DMA((3,)),
        ],
        compiler_params=params(8),
        cost_estimate=SHORT,
        name="own_pages",
    )(place, in_hbm(cached_len), in_hbm(page_loc), in_hbm(latent_pool))


def new_kernel(q_in, lat_in, w_in, q_out, kv_out, rope_out, q_ref, lat_ref, w_ref, sems):
    copies = [
        pltpu.make_async_copy(source, target, sems.at[k])
        for k, (source, target) in enumerate([(q_in, q_ref), (lat_in, lat_ref), (w_in, w_ref)])
    ]
    for copy in copies:
        copy.start()
    lane = lax.broadcasted_iota(jnp.int32, (NEW, 128), 1)
    copies[0].wait()
    for pair in range(HPD // 2):
        two = q_ref[:, 384 * pair : 384 * (pair + 1)].astype(F32)
        for odd in range(2):
            head = 2 * pair + odd
            one = pltpu.roll(two, NOPE + ROPE, 1) if odd else two
            tail = jnp.where(lane < ROPE, one[:, NOPE : NOPE + 128], jnp.where(lane == ROPE, 1.0, 0.0))
            q_out[:, 256 * head : 256 * head + 128] = one[:, :NOPE].astype(BF)
            q_out[:, 256 * head + 128 : 256 * head + 256] = tail.astype(BF)
    copies[1].wait()
    rope = jnp.concatenate([lat_ref[KV:, :].astype(F32), jnp.zeros((128 - ROPE, NEW), F32)], 0)
    rope_out[...] = rope.T.astype(BF)
    latent = lat_ref[:KV, :].astype(F32).T.astype(BF)
    copies[2].wait()
    kv_out[...] = jnp.dot(latent, w_ref[...], preferred_element_type=F32).astype(BF)


def new_tokens(queries, latent_t, w_ukv):
    operands = queries, latent_t, w_ukv
    return pl.pallas_call(
        new_kernel,
        out_shape=[
            jax.ShapeDtypeStruct((NEW, HPD * 256), BF),
            jax.ShapeDtypeStruct((NEW, HPD * 256), BF),
            jax.ShapeDtypeStruct((NEW, 128), BF),
        ],
        in_specs=[pl.BlockSpec(memory_space=pltpu.HBM)] * 3,
        out_specs=[VMEM] * 3,
        scratch_shapes=[pltpu.VMEM(operand.shape, BF) for operand in operands]
        + [pltpu.SemaphoreType.DMA((3,))],
        compiler_params=params(24),
        cost_estimate=SHORT,
        name="new_tokens",
    )(*[in_hbm(operand) for operand in operands])


def lift_kernel(count, *refs):
    w_ref = refs[count]
    kv_out, rope_out = refs[count + 1 :]
    for i in range(count):
        rows = refs[i].shape[0]
        kv_out[rows * i : rows * (i + 1), :] = jnp.dot(
            refs[i][:, :KV], w_ref[...], preferred_element_type=F32
        ).astype(BF)
        rope_out[rows * i : rows * (i + 1), :] = refs[i][:, KV:]


def lift(pieces, w_ukv):
    count = len(pieces)
    rows = count * pieces[0].shape[0]
    return pl.pallas_call(
        functools.partial(lift_kernel, count),
        out_shape=[
            jax.ShapeDtypeStruct((rows, HPD * 256), BF),
            jax.ShapeDtypeStruct((rows, 128), BF),
        ],
        in_specs=[VMEM] * (count + 1),
        out_specs=[VMEM] * 2,
        compiler_params=params(24),
        cost_estimate=SHORT,
        name="lift",
    )(*pieces, w_ukv)


def group_scores(q, kv, rope):
    keys = jnp.concatenate([kv[:, :NOPE], rope], 1)
    return lax.dot_general(q, keys, NT, preferred_element_type=F32)


def group_sum(weight, kv):
    values = jnp.concatenate([kv[:, NOPE:], jnp.ones((kv.shape[0], 128), BF)], 1)
    return jnp.dot(weight, values, preferred_element_type=F32)


LARGE = 2.0**60


def weights_of(s, top):
    return jnp.exp2((s - top) * SCALE).astype(BF)


def row_max(s):
    return jnp.max(s, axis=1, keepdims=True)


def new_scores(half, q, kv_new, rope_new):
    count = HALF * (half + 1)
    n = group_scores(q, kv_new[:count, :], rope_new[:count, :])
    key = lax.broadcasted_iota(jnp.int32, n.shape, 1)
    row = lax.broadcasted_iota(jnp.int32, n.shape, 0) + half * HALF
    return jnp.where(key <= row, n, BLOCKED)


def columns(h, width):
    if isinstance(h, int):
        return slice(h * width, (h + 1) * width)
    return pl.ds(pl.multiple_of(h * width, width), width)


def near_kernel(
    place, q_ref, kv_ref, rope_ref, kv_new, rope_new, w_in, sum_ref, top_ref, keep_ref, give_ref, w_ref, turned, sems
):
    head_id = place[1]
    core = head_id & 1
    x = lax.shift_right_logical(head_id, 1) & (SIDE - 1)
    y = lax.shift_right_logical(head_id, 3)
    width = 2 * SIDE * COLS
    copies = [
        pltpu.make_async_copy(
            w_in.at[:, pl.ds(pl.multiple_of(((y + dy) & (SIDE - 1)) * width, 256), width)],
            w_ref.at[dy],
            sems.at[dy],
        )
        for dy in range(SIDE)
    ]
    for copy in copies:
        copy.start()

    def work(h, exact):
        head = columns(h, 256)
        kv = kv_ref[:, head]
        for half in range(2):
            rows = slice(half * HALF, (half + 1) * HALF)
            count = HALF * (half + 1)
            q = q_ref[rows, head]
            new = kv_new[:count, head]
            n = new_scores(half, q, new, rope_new)
            s = group_scores(q, kv, rope_ref[...])
            if exact:
                top = jnp.maximum(row_max(n), row_max(s))
            else:
                own_keys = jnp.concatenate([new[half * HALF :, :NOPE], rope_new[rows, :]], 1)
                top = jnp.sum(q.astype(F32) * own_keys.astype(F32), axis=1, keepdims=True)
            sum_ref[rows, head] = group_sum(weights_of(s, top), kv) + group_sum(weights_of(n, top), new)
            top_ref[rows, columns(h, 128)] = jnp.broadcast_to(top, (HALF, 128))

    def turn(dy):
        for k in range(width // 256):
            turned[256 * k : 256 * (k + 1), :] = w_ref[dy, :, 256 * k : 256 * (k + 1)].T
        for dx in range(SIDE):
            at = ((x + dx) & (SIDE - 1)) * 2
            mine = (jnp.where(core == 0, dx, dy), (jnp.where(core == 0, dy, dx) + 3) & (SIDE - 1))
            theirs = (jnp.where(core == 0, dy, dx), (jnp.where(core == 0, dx, dy) + 3) & (SIDE - 1))
            keep_ref[mine] = turned[pl.ds(pl.multiple_of((at + core) * COLS, 32), COLS), :]
            give_ref[theirs] = turned[pl.ds(pl.multiple_of((at + 1 - core) * COLS, 32), COLS), :]

    for h in range(HPD):
        work(h, False)
        copies[h].wait()
        turn(h)

    worst = functools.reduce(jnp.maximum, [sum_ref[:, 256 * h + VD : 256 * (h + 1)] for h in range(HPD)])

    @pl.when(jnp.logical_not(jnp.max(worst) < LARGE))
    def _():
        lax.fori_loop(0, HPD, lambda h, carry: work(h, True), None)


def attend_near(place, q_ext, kv, rope, kv_new, rope_new, w_out):
    rows = HPD * VD
    part = jax.ShapeDtypeStruct((SIDE, SIDE, COLS, rows), BF)
    return pl.pallas_call(
        near_kernel,
        out_shape=[
            jax.ShapeDtypeStruct((NEW, HPD * 256), F32),
            jax.ShapeDtypeStruct((NEW, HPD * 128), F32),
            part,
            part,
        ],
        in_specs=[SMEM] + [VMEM] * 5 + [pl.BlockSpec(memory_space=pltpu.HBM)],
        out_specs=[VMEM] * 4,
        scratch_shapes=[
            pltpu.VMEM((SIDE, rows, 2 * SIDE * COLS), BF),
            pltpu.VMEM((2 * SIDE * COLS, rows), BF),
            pltpu.SemaphoreType.DMA((SIDE,)),
        ],
        compiler_params=params(28),
        cost_estimate=SHORT,
        name="attend_near",
    )(place, q_ext, kv, rope, kv_new, rope_new, in_hbm(w_out))


def far_kernel(groups, q_ref, sum_ref, top_ref, *refs):
    out_ref, total_ref = refs[-2:]

    def work(h, exact):
        head = columns(h, 256)
        q = q_ref[:, head]
        top = top_ref[:, columns(h, 128)][:, :1]
        total = sum_ref[:, head]
        if exact:
            scores = [group_scores(q, refs[2 * g][:, head], refs[2 * g + 1][...]) for g in range(groups)]
            old = top
            top = functools.reduce(jnp.maximum, [row_max(s) for s in scores] + [old])
            total = total * jnp.exp2((old - top) * SCALE)
        for g in range(groups):
            kv = refs[2 * g][:, head]
            s = scores[g] if exact else group_scores(q, kv, refs[2 * g + 1][...])
            total = total + group_sum(weights_of(s, top), kv)
        total_ref[:, head] = total

    for h in range(HPD):
        work(h, False)
    worst = functools.reduce(jnp.maximum, [total_ref[:, 256 * h + VD : 256 * (h + 1)] for h in range(HPD)])

    @pl.when(jnp.logical_not(jnp.max(worst) < LARGE))
    def _():
        lax.fori_loop(0, HPD, lambda h, carry: work(h, True), None)

    for h in range(HPD):
        total = total_ref[:, columns(h, 256)]
        out_ref[:, columns(h, VD)] = (total[:, :VD] / total[:, VD:]).astype(BF)


def attend_far(q_ext, sums, tops, far):
    operands = [array for pair in far for array in pair]
    return pl.pallas_call(
        functools.partial(far_kernel, len(far)),
        out_shape=jax.ShapeDtypeStruct((NEW, HPD * VD), BF),
        in_specs=[VMEM] * (3 + len(operands)),
        out_specs=VMEM,
        scratch_shapes=[pltpu.VMEM((NEW, HPD * 256), F32)],
        compiler_params=params(24),
        cost_estimate=LONG,
        name="attend_far",
    )(q_ext, sums, tops, *operands)


def project_kernel(att_ref, other_ref, keep_ref, got_ref, out_ref):
    rows = out_ref.shape[0] * COLS
    out = lax.dot_general(
        keep_ref[...].reshape(rows, HPD * VD), att_ref[...], NT, preferred_element_type=F32
    ) + lax.dot_general(
        got_ref[...].reshape(rows, HPD * VD), other_ref[...], NT, preferred_element_type=F32
    )
    out_ref[...] = out.reshape(out_ref.shape).astype(BF)


def project(a, first, count, att, other, keep, got):
    spec = pl.BlockSpec((1, count, COLS, HPD * VD), lambda i: (a, first // count, 0, 0))
    whole = pl.BlockSpec((NEW, HPD * VD), lambda i: (0, 0))
    return pl.pallas_call(
        project_kernel,
        out_shape=jax.ShapeDtypeStruct((count, COLS, NEW), BF),
        grid=(1,),
        in_specs=[whole, whole, spec, spec],
        out_specs=pl.BlockSpec((count, COLS, NEW), lambda i: (0, 0, 0)),
        compiler_params=params(16),
        cost_estimate=SHORT,
        name="project",
    )(att, other, keep, got)


def add(*terms):
    total = terms[0].astype(F32)
    for term in terms[1:]:
        total = total + term.astype(F32)
    return total.astype(BF)


def per_device(queries, new_latent, latent_pool, w_ukv, w_out, cached_len, page_loc):
    place = jnp.stack([lax.axis_index("pool"), lax.axis_index(PLANE)]).astype(jnp.int32)
    outgoing = own_pages(place, cached_len, page_loc, latent_pool)
    arrived = lax.all_to_all(outgoing, "pool", split_axis=0, concat_axis=0, tiled=True)
    own = arrived.reshape(REQ * PAGE, PAY)
    own, new_latent = lax.optimization_barrier((own, new_latent))
    q_ext, kv_new, rope_new = new_tokens(queries, new_latent.T, w_ukv)
    line = [own, send_first(own, 2), send_first(own, 1), send_first(own, -1)]
    *line, kv_new = lax.optimization_barrier((*line, kv_new))
    line = jnp.concatenate(line, 0)
    pieces = [send_second(line, d) for d in (2, 1, -1)]
    near = lift([line, swap(line)], w_ukv)
    sums, tops, keep, give = attend_near(place, q_ext, *near, kv_new, rope_new, w_out)
    got = swap(give)
    *pieces, sums = lax.optimization_barrier((*pieces, sums))
    far = [lift(pieces, w_ukv), lift([swap(piece) for piece in pieces], w_ukv)]
    att = attend_far(q_ext, sums, tops, far)
    other = swap(att)
    def partial_sums(a, half):
        return project(a, 2 * half, 2, att, other, keep, got)

    far_parts = [partial_sums(2, half) for half in range(2)]
    att, far_parts[1] = lax.optimization_barrier((att, far_parts[1]))
    passing = send_first(far_parts[0], 1), send_first(far_parts[1], -1)
    early = send_first(partial_sums(1, 1), 1), send_first(partial_sums(3, 0), -1)
    late = (
        send_first(add(partial_sums(1, 0), passing[0]), 1),
        send_first(add(partial_sums(3, 1), passing[1]), -1),
    )
    one, two = add(partial_sums(0, 0), late[0], early[1])
    rest = partial_sums(0, 1), early[0], late[1]
    three = add(*[value[0] for value in rest])
    moved = [send_second(two, 2), send_second(one, 1), send_second(three, -1)]
    out = add(*[value[1] for value in rest], *moved)
    return out.T


def solution(mesh):
    fine = jax.sharding.Mesh(
        mesh.devices.reshape(mesh.shape["pool"], 2, 2, 2, 2, 2), ("pool",) + PLANE
    )
    placed = (
        P("pool", PLANE),
        P("pool", None),
        P(("pool",) + PLANE, None),
        P(None, PLANE),
        P(PLANE, None),
        P(),
        P(),
    )
    return jax.shard_map(
        per_device, mesh=fine, in_specs=placed, out_specs=P("pool", PLANE), check_vma=False
    )
```

```python
import functools

import jax
import jax.numpy as jnp
from jax import lax
from jax.experimental import pallas as pl
from jax.experimental.pallas import tpu as pltpu
from jax.sharding import PartitionSpec as P

NOPE = 128
ROPE = 64
VD = 128
KV = 512
NEW = 512
PAGE = 8
MAXP = 256
HPD = 4
REQ = 8
N_HEAD = 32
PAGES_DEV = 16
D = 7168
COLS = D // N_HEAD
WIDTH = KV + ROPE
PAY = KV + 128
HALF = NEW // 2
SIDE = 4
BLOCKED = -1e30
SCALE = (NOPE + ROPE) ** -0.5 * 1.4426950408889634
BF = jnp.bfloat16
F32 = jnp.float32
NT = (((1,), (1,)), ((), ()))
VMEM = pl.BlockSpec(memory_space=pltpu.VMEM)
SMEM = pl.BlockSpec(memory_space=pltpu.SMEM)


PLANE = ("y_hi", "y_lo", "x_hi", "x_lo", "core")


def plane_perm(move):
    def index(y, x, c):
        return ((y % SIDE) * SIDE + x % SIDE) * 2 + c

    return [
        (index(y, x, c), index(*move(y, x, c)))
        for y in range(SIDE)
        for x in range(SIDE)
        for c in range(2)
    ]


SWAP = plane_perm(lambda y, x, c: (y, x, 1 - c))


def send_first(value, d):
    perm = plane_perm(lambda y, x, c: (y + d * c, x + d * (1 - c), c))
    return lax.ppermute(value, PLANE, perm)


def send_second(value, d):
    perm = plane_perm(lambda y, x, c: (y + d * (1 - c), x + d * c, c))
    return lax.ppermute(value, PLANE, perm)


def swap(value):
    return lax.ppermute(value, PLANE, SWAP)


def in_hbm(value):
    return pltpu.with_memory_space_constraint(value, pltpu.HBM)


def params(mib):
    return pltpu.CompilerParams(vmem_limit_bytes=mib << 20)


SHORT = pl.CostEstimate(flops=0, bytes_accessed=1024, transcendentals=0)
LONG = pl.CostEstimate(flops=10**11, bytes_accessed=1024, transcendentals=0)


def pages_kernel(place, lens_in, locs_in, pool_in, out_ref, lens, locs, pool_ref, wide, chosen, rows, sems):
    copies = [
        pltpu.make_async_copy(source, target, sems.at[k])
        for k, (source, target) in enumerate([(lens_in, lens), (locs_in, locs), (pool_in, pool_ref)])
    ]
    for copy in copies:
        copy.start()
    copies[0].wait()
    copies[1].wait()
    pool_id = place[0]
    head_id = place[1]
    request = lax.broadcasted_iota(jnp.int32, (REQ, 128), 0)
    lane = lax.broadcasted_iota(jnp.int32, (REQ, 128), 1)
    past = jnp.zeros((REQ, 128), jnp.int32)
    picks = []
    for r in range(REQ):
        sel = jnp.int32(0)
        slot = jnp.int32(0)
        for i in range(MAXP // N_HEAD):
            loc = locs[r, head_id + i * N_HEAD]
            mine = lax.shift_right_logical(loc, 9) == pool_id
            sel = jnp.where(mine, loc & (PAGES_DEV - 1), sel)
            slot = jnp.where(mine, head_id + i * N_HEAD, slot)
        picks.append(sel)
        past = jnp.where(request == r, slot * PAGE - lens[r], past)
    copies[2].wait()
    wide[...] = pool_ref[...].astype(F32)
    for r in range(REQ):
        chosen[r : r + 1, :] = wide[pl.ds(picks[r], 1), :]
    for u in range(PAGE // 2):
        two = chosen[:, 2 * WIDTH * u : 2 * WIDTH * (u + 1)]
        for odd in range(2):
            t = 2 * u + odd
            token = pltpu.roll(two, WIDTH, 1) if odd else two
            extra = jnp.where(past + t < 0, 0.0, BLOCKED)
            tail = jnp.where(lane < ROPE, token[:, KV:PAY], jnp.where(lane == ROPE, extra, 0.0))
            for k in range(PAY // 128):
                part = token[:, 128 * k : 128 * (k + 1)] if 128 * k < KV else tail
                rows[k, pl.ds(t, REQ, stride=PAGE), :] = part
    for k in range(PAY // 128):
        out_ref[:, :, 128 * k : 128 * (k + 1)] = rows[k].reshape(REQ, PAGE, 128).astype(BF)


def own_pages(place, cached_len, page_loc, latent_pool):
    return pl.pallas_call(
        pages_kernel,
        out_shape=jax.ShapeDtypeStruct((REQ, PAGE, PAY), BF),
        in_specs=[SMEM] + [pl.BlockSpec(memory_space=pltpu.HBM)] * 3,
        out_specs=VMEM,
        scratch_shapes=[
            pltpu.SMEM((REQ,), jnp.int32),
            pltpu.SMEM((REQ, MAXP), jnp.int32),
            pltpu.VMEM((PAGES_DEV, PAGE * WIDTH), BF),
            pltpu.VMEM((PAGES_DEV, PAGE * WIDTH), F32),
            pltpu.VMEM((REQ, PAGE * WIDTH), F32),
            pltpu.VMEM((PAY // 128, REQ * PAGE, 128), F32),
            pltpu.SemaphoreType.DMA((3,)),
        ],
        compiler_params=params(8),
        cost_estimate=SHORT,
        name="own_pages",
    )(place, in_hbm(cached_len), in_hbm(page_loc), in_hbm(latent_pool))


def new_kernel(q_in, lat_in, w_in, q_out, kv_out, rope_out, q_ref, lat_ref, w_ref, sems):
    copies = [
        pltpu.make_async_copy(source, target, sems.at[k])
        for k, (source, target) in enumerate([(q_in, q_ref), (lat_in, lat_ref), (w_in, w_ref)])
    ]
    for copy in copies:
        copy.start()
    lane = lax.broadcasted_iota(jnp.int32, (NEW, 128), 1)
    copies[0].wait()
    for pair in range(HPD // 2):
        two = q_ref[:, 384 * pair : 384 * (pair + 1)].astype(F32)
        for odd in range(2):
            head = 2 * pair + odd
            one = pltpu.roll(two, NOPE + ROPE, 1) if odd else two
            tail = jnp.where(lane < ROPE, one[:, NOPE : NOPE + 128], jnp.where(lane == ROPE, 1.0, 0.0))
            q_out[:, 256 * head : 256 * head + 128] = one[:, :NOPE].astype(BF)
            q_out[:, 256 * head + 128 : 256 * head + 256] = tail.astype(BF)
    copies[1].wait()
    rope = jnp.concatenate([lat_ref[KV:, :].astype(F32), jnp.zeros((128 - ROPE, NEW), F32)], 0)
    rope_out[...] = rope.T.astype(BF)
    latent = lat_ref[:KV, :].astype(F32).T.astype(BF)
    copies[2].wait()
    kv_out[...] = jnp.dot(latent, w_ref[...], preferred_element_type=F32).astype(BF)


def new_tokens(queries, latent_t, w_ukv):
    operands = queries, latent_t, w_ukv
    return pl.pallas_call(
        new_kernel,
        out_shape=[
            jax.ShapeDtypeStruct((NEW, HPD * 256), BF),
            jax.ShapeDtypeStruct((NEW, HPD * 256), BF),
            jax.ShapeDtypeStruct((NEW, 128), BF),
        ],
        in_specs=[pl.BlockSpec(memory_space=pltpu.HBM)] * 3,
        out_specs=[VMEM] * 3,
        scratch_shapes=[pltpu.VMEM(operand.shape, BF) for operand in operands]
        + [pltpu.SemaphoreType.DMA((3,))],
        compiler_params=params(24),
        cost_estimate=SHORT,
        name="new_tokens",
    )(*[in_hbm(operand) for operand in operands])


def lift_into(pieces, w_ref, kv_ref, rope_ref):
    for i, piece in enumerate(pieces):
        rows = slice(piece.shape[0] * i, piece.shape[0] * (i + 1))
        kv_ref[rows, :] = jnp.dot(piece[:, :KV], w_ref[...], preferred_element_type=F32).astype(BF)
        rope_ref[rows, :] = piece[:, KV:]


def lift_kernel(count, *refs):
    lift_into(refs[:count], *refs[count:])


def lift(pieces, w_ukv):
    count = len(pieces)
    rows = count * pieces[0].shape[0]
    return pl.pallas_call(
        functools.partial(lift_kernel, count),
        out_shape=[
            jax.ShapeDtypeStruct((rows, HPD * 256), BF),
            jax.ShapeDtypeStruct((rows, 128), BF),
        ],
        in_specs=[VMEM] * (count + 1),
        out_specs=[VMEM] * 2,
        compiler_params=params(24),
        cost_estimate=SHORT,
        name="lift",
    )(*pieces, w_ukv)


def group_scores(q, kv, rope):
    keys = jnp.concatenate([kv[:, :NOPE], rope], 1)
    return lax.dot_general(q, keys, NT, preferred_element_type=F32)


def group_sum(weight, kv):
    values = jnp.concatenate([kv[:, NOPE:], jnp.ones((kv.shape[0], 128), BF)], 1)
    return jnp.dot(weight, values, preferred_element_type=F32)


LARGE = 2.0**60


def weights_of(s, top):
    return jnp.exp2((s - top) * SCALE).astype(BF)


def row_max(s):
    return jnp.max(s, axis=1, keepdims=True)


def new_scores(half, q, kv_new, rope_new):
    count = HALF * (half + 1)
    n = group_scores(q, kv_new[:count, :], rope_new[:count, :])
    key = lax.broadcasted_iota(jnp.int32, n.shape, 1)
    row = lax.broadcasted_iota(jnp.int32, n.shape, 0) + half * HALF
    return jnp.where(key <= row, n, BLOCKED)


def columns(h, width):
    if isinstance(h, int):
        return slice(h * width, (h + 1) * width)
    return pl.ds(pl.multiple_of(h * width, width), width)


def near_kernel(
    place, q_ref, line_ref, other_ref, up_ref, kv_new, rope_new, w_in,
    sum_ref, top_ref, keep_ref, give_ref,
    kv_ref, rope_ref, w_ref, turned, sems,
):
    head_id = place[1]
    core = head_id & 1
    x = lax.shift_right_logical(head_id, 1) & (SIDE - 1)
    y = lax.shift_right_logical(head_id, 3)
    width = 2 * SIDE * COLS
    copies = [
        pltpu.make_async_copy(
            w_in.at[:, pl.ds(pl.multiple_of(((y + dy) & (SIDE - 1)) * width, 256), width)],
            w_ref.at[dy],
            sems.at[dy],
        )
        for dy in range(SIDE)
    ]
    for copy in copies:
        copy.start()
    lift_into((line_ref, other_ref), up_ref, kv_ref, rope_ref)

    def work(h, exact):
        head = columns(h, 256)
        kv = kv_ref[:, head]
        for half in range(2):
            rows = slice(half * HALF, (half + 1) * HALF)
            count = HALF * (half + 1)
            q = q_ref[rows, head]
            new = kv_new[:count, head]
            n = new_scores(half, q, new, rope_new)
            s = group_scores(q, kv, rope_ref[...])
            if exact:
                top = jnp.maximum(row_max(n), row_max(s))
            else:
                own_keys = jnp.concatenate([new[half * HALF :, :NOPE], rope_new[rows, :]], 1)
                top = jnp.sum(q.astype(F32) * own_keys.astype(F32), axis=1, keepdims=True)
            sum_ref[rows, head] = group_sum(weights_of(s, top), kv) + group_sum(weights_of(n, top), new)
            top_ref[rows, columns(h, 128)] = jnp.broadcast_to(top, (HALF, 128))

    def turn(dy):
        for k in range(width // 256):
            turned[256 * k : 256 * (k + 1), :] = w_ref[dy, :, 256 * k : 256 * (k + 1)].T
        for dx in range(SIDE):
            at = ((x + dx) & (SIDE - 1)) * 2
            mine = (jnp.where(core == 0, dx, dy), (jnp.where(core == 0, dy, dx) + 3) & (SIDE - 1))
            theirs = (jnp.where(core == 0, dy, dx), (jnp.where(core == 0, dx, dy) + 3) & (SIDE - 1))
            keep_ref[mine] = turned[pl.ds(pl.multiple_of((at + core) * COLS, 32), COLS), :]
            give_ref[theirs] = turned[pl.ds(pl.multiple_of((at + 1 - core) * COLS, 32), COLS), :]

    for h in range(HPD):
        work(h, False)
        copies[h].wait()
        turn(h)

    worst = functools.reduce(jnp.maximum, [sum_ref[:, 256 * h + VD : 256 * (h + 1)] for h in range(HPD)])

    @pl.when(jnp.logical_not(jnp.max(worst) < LARGE))
    def _():
        lax.fori_loop(0, HPD, lambda h, carry: work(h, True), None)


def attend_near(place, q_ext, line, other, w_ukv, kv_new, rope_new, w_out):
    rows = HPD * VD
    part = jax.ShapeDtypeStruct((SIDE, SIDE, COLS, rows), BF)
    return pl.pallas_call(
        near_kernel,
        out_shape=[
            jax.ShapeDtypeStruct((NEW, HPD * 256), F32),
            jax.ShapeDtypeStruct((NEW, HPD * 128), F32),
            part,
            part,
        ],
        in_specs=[SMEM] + [VMEM] * 6 + [pl.BlockSpec(memory_space=pltpu.HBM)],
        out_specs=[VMEM] * 4,
        scratch_shapes=[
            pltpu.VMEM((2 * line.shape[0], HPD * 256), BF),
            pltpu.VMEM((2 * line.shape[0], 128), BF),
            pltpu.VMEM((SIDE, rows, 2 * SIDE * COLS), BF),
            pltpu.VMEM((2 * SIDE * COLS, rows), BF),
            pltpu.SemaphoreType.DMA((SIDE,)),
        ],
        compiler_params=params(28),
        cost_estimate=SHORT,
        name="attend_near",
    )(place, q_ext, line, other, w_ukv, kv_new, rope_new, in_hbm(w_out))


def far_kernel(
    q_ref, sum_ref, top_ref, kv_ref, rope_ref, up_ref, piece_0, piece_1, piece_2, out_ref, total_ref, kv_more, rope_more
):
    lift_into((piece_0, piece_1, piece_2), up_ref, kv_more, rope_more)
    groups = (kv_ref, rope_ref), (kv_more, rope_more)

    def work(h, exact):
        head = columns(h, 256)
        q = q_ref[:, head]
        top = top_ref[:, columns(h, 128)][:, :1]
        total = sum_ref[:, head]
        if exact:
            scores = [group_scores(q, kv[:, head], rope[...]) for kv, rope in groups]
            old = top
            top = functools.reduce(jnp.maximum, [row_max(s) for s in scores] + [old])
            total = total * jnp.exp2((old - top) * SCALE)
        for g, (kv, rope) in enumerate(groups):
            s = scores[g] if exact else group_scores(q, kv[:, head], rope[...])
            total = total + group_sum(weights_of(s, top), kv[:, head])
        total_ref[:, head] = total

    for h in range(HPD):
        work(h, False)
    worst = functools.reduce(jnp.maximum, [total_ref[:, 256 * h + VD : 256 * (h + 1)] for h in range(HPD)])

    @pl.when(jnp.logical_not(jnp.max(worst) < LARGE))
    def _():
        lax.fori_loop(0, HPD, lambda h, carry: work(h, True), None)

    for h in range(HPD):
        total = total_ref[:, columns(h, 256)]
        out_ref[:, columns(h, VD)] = (total[:, :VD] / total[:, VD:]).astype(BF)


def attend_far(q_ext, sums, tops, kv, rope, w_ukv, pieces):
    return pl.pallas_call(
        far_kernel,
        out_shape=jax.ShapeDtypeStruct((NEW, HPD * VD), BF),
        in_specs=[VMEM] * (6 + len(pieces)),
        out_specs=VMEM,
        scratch_shapes=[
            pltpu.VMEM((NEW, HPD * 256), F32),
            pltpu.VMEM(kv.shape, BF),
            pltpu.VMEM(rope.shape, BF),
        ],
        compiler_params=params(24),
        cost_estimate=LONG,
        name="attend_far",
    )(q_ext, sums, tops, kv, rope, w_ukv, *pieces)


def project_kernel(a, half, att_ref, other_ref, keep_ref, got_ref, out_ref):
    rows = 2 * COLS
    blocks = slice(2 * half, 2 * half + 2)
    out = lax.dot_general(
        keep_ref[a, blocks].reshape(rows, HPD * VD), att_ref[...], NT, preferred_element_type=F32
    ) + lax.dot_general(
        got_ref[a, blocks].reshape(rows, HPD * VD), other_ref[...], NT, preferred_element_type=F32
    )
    out_ref[...] = out.reshape(out_ref.shape).astype(BF)


def project(a, half, att, other, keep, got):
    return pl.pallas_call(
        functools.partial(project_kernel, a, half),
        out_shape=jax.ShapeDtypeStruct((2, COLS, NEW), BF),
        in_specs=[VMEM] * 4,
        out_specs=VMEM,
        compiler_params=params(16),
        cost_estimate=SHORT,
        name="project",
    )(att, other, keep, got)


def add(*terms):
    total = terms[0].astype(F32)
    for term in terms[1:]:
        total = total + term.astype(F32)
    return total.astype(BF)


def per_device(queries, new_latent, latent_pool, w_ukv, w_out, cached_len, page_loc):
    place = jnp.stack([lax.axis_index("pool"), lax.axis_index(PLANE)]).astype(jnp.int32)
    outgoing = own_pages(place, cached_len, page_loc, latent_pool)
    arrived = lax.all_to_all(outgoing, "pool", split_axis=0, concat_axis=0, tiled=True)
    own = arrived.reshape(REQ * PAGE, PAY)
    own, new_latent = lax.optimization_barrier((own, new_latent))
    q_ext, kv_new, rope_new = new_tokens(queries, new_latent.T, w_ukv)
    line = [own, send_first(own, 2), send_first(own, 1), send_first(own, -1)]
    *line, kv_new = lax.optimization_barrier((*line, kv_new))
    line = jnp.concatenate(line, 0)
    pieces = [send_second(line, d) for d in (2, 1, -1)]
    sums, tops, keep, give = attend_near(place, q_ext, line, swap(line), w_ukv, kv_new, rope_new, w_out)
    got = swap(give)
    *pieces, sums = lax.optimization_barrier((*pieces, sums))
    swapped = [swap(piece) for piece in pieces]
    att = attend_far(q_ext, sums, tops, *lift(pieces, w_ukv), w_ukv, swapped)
    other = swap(att)
    def partial_sums(a, half):
        return project(a, half, att, other, keep, got)

    far_parts = [partial_sums(2, half) for half in (1, 0)]
    att, far_parts[1] = lax.optimization_barrier((att, far_parts[1]))
    high, low = send_first(far_parts[0], -1), send_first(far_parts[1], 1)
    early_down, early_up = send_first(partial_sums(3, 0), -1), send_first(partial_sums(1, 1), 1)
    late_down = send_first(add(partial_sums(3, 1), high), -1)
    late_up = send_first(add(partial_sums(1, 0), low), 1)
    rest = partial_sums(0, 1), early_up, late_down
    three = add(*[value[0] for value in rest])
    one, two = add(partial_sums(0, 0), late_up, early_down)
    moved = [send_second(three, -1), send_second(two, 2), send_second(one, 1)]
    out = add(*[value[1] for value in rest], *moved)
    return out.T


def solution(mesh):
    fine = jax.sharding.Mesh(
        mesh.devices.reshape(mesh.shape["pool"], 2, 2, 2, 2, 2), ("pool",) + PLANE
    )
    placed = (
        P("pool", PLANE),
        P("pool", None),
        P(("pool",) + PLANE, None),
        P(None, PLANE),
        P(PLANE, None),
        P(),
        P(),
    )
    return jax.shard_map(
        per_device, mesh=fine, in_specs=placed, out_specs=P("pool", PLANE), check_vma=False
    )
```

```python
import functools

import jax
import jax.numpy as jnp
from jax import lax
from jax.experimental import pallas as pl
from jax.experimental.pallas import tpu as pltpu
from jax.sharding import PartitionSpec as P

NOPE = 128
ROPE = 64
VD = 128
KV = 512
NEW = 512
PAGE = 8
MAXP = 256
HPD = 4
REQ = 8
N_HEAD = 32
PAGES_DEV = 16
D = 7168
COLS = D // N_HEAD
WIDTH = KV + ROPE
PAY = KV + 128
HALF = NEW // 2
SIDE = 4
BLOCKED = -1e30
SCALE = (NOPE + ROPE) ** -0.5 * 1.4426950408889634
BF = jnp.bfloat16
F32 = jnp.float32
NT = (((1,), (1,)), ((), ()))
VMEM = pl.BlockSpec(memory_space=pltpu.VMEM)
SMEM = pl.BlockSpec(memory_space=pltpu.SMEM)


PLANE = ("y_hi", "y_lo", "x_hi", "x_lo", "core")


def plane_perm(move):
    def index(y, x, c):
        return ((y % SIDE) * SIDE + x % SIDE) * 2 + c

    return [
        (index(y, x, c), index(*move(y, x, c)))
        for y in range(SIDE)
        for x in range(SIDE)
        for c in range(2)
    ]


SWAP = plane_perm(lambda y, x, c: (y, x, 1 - c))


def send_first(value, d):
    perm = plane_perm(lambda y, x, c: (y + d * c, x + d * (1 - c), c))
    return lax.ppermute(value, PLANE, perm)


def send_second(value, d):
    perm = plane_perm(lambda y, x, c: (y + d * (1 - c), x + d * c, c))
    return lax.ppermute(value, PLANE, perm)


def swap(value):
    return lax.ppermute(value, PLANE, SWAP)


def in_hbm(value):
    return pltpu.with_memory_space_constraint(value, pltpu.HBM)


def params(mib):
    return pltpu.CompilerParams(vmem_limit_bytes=mib << 20)


SHORT = pl.CostEstimate(flops=0, bytes_accessed=1024, transcendentals=0)
LONG = pl.CostEstimate(flops=10**11, bytes_accessed=1024, transcendentals=0)


def pages_kernel(place, lens_in, locs_in, pool_in, out_ref, lens, locs, pool_ref, wide, chosen, rows, sems):
    copies = [
        pltpu.make_async_copy(source, target, sems.at[k])
        for k, (source, target) in enumerate([(lens_in, lens), (locs_in, locs), (pool_in, pool_ref)])
    ]
    for copy in copies:
        copy.start()
    copies[0].wait()
    copies[1].wait()
    pool_id = place[0]
    head_id = place[1]
    request = lax.broadcasted_iota(jnp.int32, (REQ, 128), 0)
    lane = lax.broadcasted_iota(jnp.int32, (REQ, 128), 1)
    past = jnp.zeros((REQ, 128), jnp.int32)
    picks = []
    for r in range(REQ):
        sel = jnp.int32(0)
        slot = jnp.int32(0)
        for i in range(MAXP // N_HEAD):
            loc = locs[r, head_id + i * N_HEAD]
            mine = lax.shift_right_logical(loc, 9) == pool_id
            sel = jnp.where(mine, loc & (PAGES_DEV - 1), sel)
            slot = jnp.where(mine, head_id + i * N_HEAD, slot)
        picks.append(sel)
        past = jnp.where(request == r, slot * PAGE - lens[r], past)
    copies[2].wait()
    wide[...] = pool_ref[...].astype(F32)
    for r in range(REQ):
        chosen[r : r + 1, :] = wide[pl.ds(picks[r], 1), :]
    for u in range(PAGE // 2):
        two = chosen[:, 2 * WIDTH * u : 2 * WIDTH * (u + 1)]
        for odd in range(2):
            t = 2 * u + odd
            token = pltpu.roll(two, WIDTH, 1) if odd else two
            extra = jnp.where(past + t < 0, 0.0, BLOCKED)
            tail = jnp.where(lane < ROPE, token[:, KV:PAY], jnp.where(lane == ROPE, extra, 0.0))
            for k in range(PAY // 128):
                part = token[:, 128 * k : 128 * (k + 1)] if 128 * k < KV else tail
                rows[k, pl.ds(t, REQ, stride=PAGE), :] = part
    for k in range(PAY // 128):
        out_ref[:, :, 128 * k : 128 * (k + 1)] = rows[k].reshape(REQ, PAGE, 128).astype(BF)


def own_pages(place, cached_len, page_loc, latent_pool):
    return pl.pallas_call(
        pages_kernel,
        out_shape=jax.ShapeDtypeStruct((REQ, PAGE, PAY), BF),
        in_specs=[SMEM] + [pl.BlockSpec(memory_space=pltpu.HBM)] * 3,
        out_specs=VMEM,
        scratch_shapes=[
            pltpu.SMEM((REQ,), jnp.int32),
            pltpu.SMEM((REQ, MAXP), jnp.int32),
            pltpu.VMEM((PAGES_DEV, PAGE * WIDTH), BF),
            pltpu.VMEM((PAGES_DEV, PAGE * WIDTH), F32),
            pltpu.VMEM((REQ, PAGE * WIDTH), F32),
            pltpu.VMEM((PAY // 128, REQ * PAGE, 128), F32),
            pltpu.SemaphoreType.DMA((3,)),
        ],
        compiler_params=params(8),
        cost_estimate=SHORT,
        name="own_pages",
    )(place, in_hbm(cached_len), in_hbm(page_loc), in_hbm(latent_pool))


def new_kernel(q_in, lat_in, w_in, q_out, kv_out, rope_out, q_ref, lat_ref, w_ref, sems):
    copies = [
        pltpu.make_async_copy(source, target, sems.at[k])
        for k, (source, target) in enumerate([(q_in, q_ref), (lat_in, lat_ref), (w_in, w_ref)])
    ]
    for copy in copies:
        copy.start()
    lane = lax.broadcasted_iota(jnp.int32, (NEW, 128), 1)
    copies[0].wait()
    for pair in range(HPD // 2):
        two = q_ref[:, 384 * pair : 384 * (pair + 1)].astype(F32)
        for odd in range(2):
            head = 2 * pair + odd
            one = pltpu.roll(two, NOPE + ROPE, 1) if odd else two
            tail = jnp.where(lane < ROPE, one[:, NOPE : NOPE + 128], jnp.where(lane == ROPE, 1.0, 0.0))
            q_out[:, 256 * head : 256 * head + 128] = one[:, :NOPE].astype(BF)
            q_out[:, 256 * head + 128 : 256 * head + 256] = tail.astype(BF)
    copies[1].wait()
    rope = jnp.concatenate([lat_ref[KV:, :].astype(F32), jnp.zeros((128 - ROPE, NEW), F32)], 0)
    rope_out[...] = rope.T.astype(BF)
    latent = lat_ref[:KV, :].astype(F32).T.astype(BF)
    copies[2].wait()
    kv_out[...] = jnp.dot(latent, w_ref[...], preferred_element_type=F32).astype(BF)


def new_tokens(queries, latent_t, w_ukv):
    operands = queries, latent_t, w_ukv
    return pl.pallas_call(
        new_kernel,
        out_shape=[
            jax.ShapeDtypeStruct((NEW, HPD * 256), BF),
            jax.ShapeDtypeStruct((NEW, HPD * 256), BF),
            jax.ShapeDtypeStruct((NEW, 128), BF),
        ],
        in_specs=[pl.BlockSpec(memory_space=pltpu.HBM)] * 3,
        out_specs=[VMEM] * 3,
        scratch_shapes=[pltpu.VMEM(operand.shape, BF) for operand in operands]
        + [pltpu.SemaphoreType.DMA((3,))],
        compiler_params=params(24),
        cost_estimate=SHORT,
        name="new_tokens",
    )(*[in_hbm(operand) for operand in operands])


def lift_into(pieces, w_ref, kv_ref, rope_ref):
    for i, piece in enumerate(pieces):
        rows = slice(piece.shape[0] * i, piece.shape[0] * (i + 1))
        kv_ref[rows, :] = jnp.dot(piece[:, :KV], w_ref[...], preferred_element_type=F32).astype(BF)
        rope_ref[rows, :] = piece[:, KV:]


def lift_kernel(count, *refs):
    lift_into(refs[:count], *refs[count:])


def lift(pieces, w_ukv):
    count = len(pieces)
    rows = count * pieces[0].shape[0]
    return pl.pallas_call(
        functools.partial(lift_kernel, count),
        out_shape=[
            jax.ShapeDtypeStruct((rows, HPD * 256), BF),
            jax.ShapeDtypeStruct((rows, 128), BF),
        ],
        in_specs=[VMEM] * (count + 1),
        out_specs=[VMEM] * 2,
        compiler_params=params(24),
        cost_estimate=SHORT,
        name="lift",
    )(*pieces, w_ukv)


def group_scores(q, kv, rope):
    keys = jnp.concatenate([kv[:, :NOPE], rope], 1)
    return lax.dot_general(q, keys, NT, preferred_element_type=F32)


def group_sum(weight, kv):
    values = jnp.concatenate([kv[:, NOPE:], jnp.ones((kv.shape[0], 128), BF)], 1)
    return jnp.dot(weight, values, preferred_element_type=F32)


LARGE = 2.0**60


def weights_of(s, top):
    return jnp.exp2((s - top) * SCALE).astype(BF)


def row_max(s):
    return jnp.max(s, axis=1, keepdims=True)


def new_scores(half, q, kv_new, rope_new):
    count = HALF * (half + 1)
    n = group_scores(q, kv_new[:count, :], rope_new[:count, :])
    key = lax.broadcasted_iota(jnp.int32, n.shape, 1)
    row = lax.broadcasted_iota(jnp.int32, n.shape, 0) + half * HALF
    return jnp.where(key <= row, n, BLOCKED)


def columns(h, width):
    if isinstance(h, int):
        return slice(h * width, (h + 1) * width)
    return pl.ds(pl.multiple_of(h * width, width), width)


def near_kernel(
    place, q_ref, line_ref, other_ref, up_ref, kv_new, rope_new, w_in,
    sum_ref, top_ref, keep_ref, give_ref,
    kv_ref, rope_ref, w_ref, turned, sems,
):
    head_id = place[1]
    core = head_id & 1
    x = lax.shift_right_logical(head_id, 1) & (SIDE - 1)
    y = lax.shift_right_logical(head_id, 3)
    width = 2 * SIDE * COLS
    copies = [
        pltpu.make_async_copy(
            w_in.at[:, pl.ds(pl.multiple_of(((y + dy) & (SIDE - 1)) * width, 256), width)],
            w_ref.at[dy],
            sems.at[dy],
        )
        for dy in range(SIDE)
    ]
    for copy in copies:
        copy.start()
    lift_into((line_ref, other_ref), up_ref, kv_ref, rope_ref)

    def work(h, exact):
        head = columns(h, 256)
        kv = kv_ref[:, head]
        for half in range(2):
            rows = slice(half * HALF, (half + 1) * HALF)
            count = HALF * (half + 1)
            q = q_ref[rows, head]
            new = kv_new[:count, head]
            n = new_scores(half, q, new, rope_new)
            s = group_scores(q, kv, rope_ref[...])
            if exact:
                top = jnp.maximum(row_max(n), row_max(s))
            else:
                own_keys = jnp.concatenate([new[half * HALF :, :NOPE], rope_new[rows, :]], 1)
                top = jnp.sum(q.astype(F32) * own_keys.astype(F32), axis=1, keepdims=True)
            sum_ref[rows, head] = group_sum(weights_of(s, top), kv) + group_sum(weights_of(n, top), new)
            top_ref[rows, columns(h, 128)] = jnp.broadcast_to(top, (HALF, 128))

    def turn(dy):
        for k in range(width // 256):
            turned[dy % 2, 256 * k : 256 * (k + 1), :] = w_ref[dy, :, 256 * k : 256 * (k + 1)].T
        for dx in range(SIDE):
            at = ((x + dx) & (SIDE - 1)) * 2
            mine = (jnp.where(core == 0, dx, dy), (jnp.where(core == 0, dy, dx) + 3) & (SIDE - 1))
            theirs = (jnp.where(core == 0, dy, dx), (jnp.where(core == 0, dx, dy) + 3) & (SIDE - 1))
            keep_ref[mine] = turned[dy % 2, pl.ds(pl.multiple_of((at + core) * COLS, 32), COLS), :]
            give_ref[theirs] = turned[dy % 2, pl.ds(pl.multiple_of((at + 1 - core) * COLS, 32), COLS), :]

    for h in range(HPD):
        work(h, False)
        copies[h].wait()
        turn(h)

    worst = functools.reduce(jnp.maximum, [sum_ref[:, 256 * h + VD : 256 * (h + 1)] for h in range(HPD)])

    @pl.when(jnp.logical_not(jnp.max(worst) < LARGE))
    def _():
        lax.fori_loop(0, HPD, lambda h, carry: work(h, True), None)


def attend_near(place, q_ext, line, other, w_ukv, kv_new, rope_new, w_out):
    rows = HPD * VD
    part = jax.ShapeDtypeStruct((SIDE, SIDE, COLS, rows), BF)
    return pl.pallas_call(
        near_kernel,
        out_shape=[
            jax.ShapeDtypeStruct((NEW, HPD * 256), F32),
            jax.ShapeDtypeStruct((NEW, HPD * 128), F32),
            part,
            part,
        ],
        in_specs=[SMEM] + [VMEM] * 6 + [pl.BlockSpec(memory_space=pltpu.HBM)],
        out_specs=[VMEM] * 4,
        scratch_shapes=[
            pltpu.VMEM((2 * line.shape[0], HPD * 256), BF),
            pltpu.VMEM((2 * line.shape[0], 128), BF),
            pltpu.VMEM((SIDE, rows, 2 * SIDE * COLS), BF),
            pltpu.VMEM((2, 2 * SIDE * COLS, rows), BF),
            pltpu.SemaphoreType.DMA((SIDE,)),
        ],
        compiler_params=params(28),
        cost_estimate=SHORT,
        name="attend_near",
    )(place, q_ext, line, other, w_ukv, kv_new, rope_new, in_hbm(w_out))


def far_kernel(
    q_ref, sum_ref, top_ref, kv_ref, rope_ref, up_ref, piece_0, piece_1, piece_2, out_ref, total_ref, kv_more, rope_more
):
    lift_into((piece_0, piece_1, piece_2), up_ref, kv_more, rope_more)
    groups = (kv_ref, rope_ref), (kv_more, rope_more)

    def work(h, exact):
        head = columns(h, 256)
        q = q_ref[:, head]
        top = top_ref[:, columns(h, 128)][:, :1]
        total = sum_ref[:, head]
        if exact:
            scores = [group_scores(q, kv[:, head], rope[...]) for kv, rope in groups]
            old = top
            top = functools.reduce(jnp.maximum, [row_max(s) for s in scores] + [old])
            total = total * jnp.exp2((old - top) * SCALE)
        for g, (kv, rope) in enumerate(groups):
            s = scores[g] if exact else group_scores(q, kv[:, head], rope[...])
            total = total + group_sum(weights_of(s, top), kv[:, head])
        total_ref[:, head] = total

    for h in range(HPD):
        work(h, False)
    worst = functools.reduce(jnp.maximum, [total_ref[:, 256 * h + VD : 256 * (h + 1)] for h in range(HPD)])

    @pl.when(jnp.logical_not(jnp.max(worst) < LARGE))
    def _():
        lax.fori_loop(0, HPD, lambda h, carry: work(h, True), None)

    for h in range(HPD):
        total = total_ref[:, columns(h, 256)]
        out_ref[:, columns(h, VD)] = (total[:, :VD] / total[:, VD:]).astype(BF)


def attend_far(q_ext, sums, tops, kv, rope, w_ukv, pieces):
    return pl.pallas_call(
        far_kernel,
        out_shape=jax.ShapeDtypeStruct((NEW, HPD * VD), BF),
        in_specs=[VMEM] * (6 + len(pieces)),
        out_specs=VMEM,
        scratch_shapes=[
            pltpu.VMEM((NEW, HPD * 256), F32),
            pltpu.VMEM(kv.shape, BF),
            pltpu.VMEM(rope.shape, BF),
        ],
        compiler_params=params(24),
        cost_estimate=LONG,
        name="attend_far",
    )(q_ext, sums, tops, kv, rope, w_ukv, *pieces)


def project_kernel(a, half, att_ref, other_ref, keep_ref, got_ref, out_ref):
    rows = 2 * COLS
    blocks = slice(2 * half, 2 * half + 2)
    out = lax.dot_general(
        keep_ref[a, blocks].reshape(rows, HPD * VD), att_ref[...], NT, preferred_element_type=F32
    ) + lax.dot_general(
        got_ref[a, blocks].reshape(rows, HPD * VD), other_ref[...], NT, preferred_element_type=F32
    )
    out_ref[...] = out.reshape(out_ref.shape).astype(BF)


def project(a, half, att, other, keep, got):
    return pl.pallas_call(
        functools.partial(project_kernel, a, half),
        out_shape=jax.ShapeDtypeStruct((2, COLS, NEW), BF),
        in_specs=[VMEM] * 4,
        out_specs=VMEM,
        compiler_params=params(16),
        cost_estimate=SHORT,
        name="project",
    )(att, other, keep, got)


def add(*terms):
    total = terms[0].astype(F32)
    for term in terms[1:]:
        total = total + term.astype(F32)
    return total.astype(BF)


def per_device(queries, new_latent, latent_pool, w_ukv, w_out, cached_len, page_loc):
    place = jnp.stack([lax.axis_index("pool"), lax.axis_index(PLANE)]).astype(jnp.int32)
    outgoing = own_pages(place, cached_len, page_loc, latent_pool)
    arrived = lax.all_to_all(outgoing, "pool", split_axis=0, concat_axis=0, tiled=True)
    own = arrived.reshape(REQ * PAGE, PAY)
    own, new_latent = lax.optimization_barrier((own, new_latent))
    q_ext, kv_new, rope_new = new_tokens(queries, new_latent.T, w_ukv)
    line = [own, send_first(own, 2), send_first(own, 1), send_first(own, -1)]
    *line, kv_new = lax.optimization_barrier((*line, kv_new))
    line = jnp.concatenate(line, 0)
    pieces = [send_second(line, d) for d in (2, 1, -1)]
    sums, tops, keep, give = attend_near(place, q_ext, line, swap(line), w_ukv, kv_new, rope_new, w_out)
    got = swap(give)
    *pieces, sums = lax.optimization_barrier((*pieces, sums))
    swapped = [swap(piece) for piece in pieces]
    att = attend_far(q_ext, sums, tops, *lift(pieces, w_ukv), w_ukv, swapped)
    other = swap(att)
    def partial_sums(a, half):
        return project(a, half, att, other, keep, got)

    far_parts = [partial_sums(2, half) for half in (1, 0)]
    att, far_parts[1] = lax.optimization_barrier((att, far_parts[1]))
    high, low = send_first(far_parts[0], -1), send_first(far_parts[1], 1)
    early_down, early_up = send_first(partial_sums(3, 0), -1), send_first(partial_sums(1, 1), 1)
    late_down = send_first(add(partial_sums(3, 1), high), -1)
    late_up = send_first(add(partial_sums(1, 0), low), 1)
    rest = partial_sums(0, 1), early_up, late_down
    three = add(*[value[0] for value in rest])
    one, two = add(partial_sums(0, 0), late_up, early_down)
    moved = [send_second(three, -1), send_second(two, 2), send_second(one, 1)]
    out = add(*[value[1] for value in rest], *moved)
    return out.T


def solution(mesh):
    fine = jax.sharding.Mesh(
        mesh.devices.reshape(mesh.shape["pool"], 2, 2, 2, 2, 2), ("pool",) + PLANE
    )
    placed = (
        P("pool", PLANE),
        P("pool", None),
        P(("pool",) + PLANE, None),
        P(None, PLANE),
        P(PLANE, None),
        P(),
        P(),
    )
    return jax.shard_map(
        per_device, mesh=fine, in_specs=placed, out_specs=P("pool", PLANE), check_vma=False
    )
```
